512 devices in a mesh: dp: 32 (over z, core), tensor: 16 (over y, x).
Axes of the slice: x: 4, y: 4, z: 16, core: 2. Of those that a mesh axis runs over, the one named last changes fastest.
Arguments:
- responses: bfloat16 [32, 1280, 4608], P('dp', 'tensor'), may hold values from -6 to 6
- kl_terms: bfloat16 [32, 8, 160], P('dp'), may hold values from -3 to 3
- norm_gain: float32 [4608], replicated, may hold values from 0.5 to 1.5
- w_qkv: bfloat16 [4608, 16, 384], P(None, 'tensor'), may hold values from -0.20623948 to 0.20623948
- readout: bfloat16 [16, 128], P('tensor'), may hold values from -0.5 to 0.5
- slot_bin: int32 [32, 8], P('dp'), may hold values from 0 to 31, as said below
- entry_source: int32 [32, 8], P('dp'), may hold values from 0 to 31, as said below
- bin_segments: int32 [32, 64], P('dp'), may hold values from 0 to 7, never falling along the last dimension, each value on 1 to 10 neighbouring positions
Outputs:
- head_outputs: bfloat16 [32, 1024, 2048], P('dp', None, 'tensor')
- scores: float32 [32, 8], P('dp')
The draws below stay inside these ranges and needn't reach their ends.
Inputs may be any that keep to these rules, and one draw needn't show every extreme that they name: Slot j of group g becomes entry j of bin slot_bin[g, j]; the slots of one group go to distinct bins. Entry j of bin b is slot j of group entry_source[b, j]; the entries of one bin come from distinct groups; slot_bin[entry_source[b, j], j] == b.
All inputs are finite; a program needn't handle non-finite values.
Results may differ from the reference program's by a relative error of at most 0.006.
The reference program's roundings to bfloat16 on the way count: a program that leaves them out, or rounds other values in their place, can miss the bound.
Values may be sent and summed in bfloat16 or wider, within the bound.
A program may use at most 64 MiB of HBM per device.

```python
import math
import jax
import jax.numpy as jnp
import numpy as np
from jax import lax

D = 4608
HD = 128
HEADS = 16
RESP = 8
CAP = 10
BIN_DEV = 64
BINS = 32
BIN_TOK = 1024
LMAX = 160
SRC_ROWS = 1280
N_TENSOR = 16


def assignment(key):
    order = jax.random.permutation(jax.random.fold_in(key, 11), BINS).astype(jnp.int32)
    shifts = jax.random.permutation(jax.random.fold_in(key, 12), BINS)[:RESP].astype(jnp.int32)
    return (order, shifts)


def draw_entry_source(key, part):
    order, shifts = assignment(key)
    bin_ids = jnp.arange(BINS, dtype=jnp.int32)
    return order[(bin_ids[:, None] + shifts[None, :]) % BINS].astype(jnp.int32)


def draw_slot_bin(key, part):
    order, shifts = assignment(key)
    inverse = jnp.argsort(order).astype(jnp.int32)
    return ((inverse[:, None] - shifts[None, :]) % BINS).astype(jnp.int32)


def draw_w_qkv(key, part):
    key = jax.random.fold_in(key, 5)
    pair_key = jax.random.fold_in(key, 2)
    value_key = jax.random.fold_in(key, 3)
    pair_part = jnp.clip(jax.random.normal(pair_key, (D, HEADS, 2 * HD), jnp.float32), -4.0, 4.0) * 1.5
    value_part = jnp.clip(jax.random.normal(value_key, (D, HEADS, HD), jnp.float32), -4.0, 4.0)
    joined = jnp.concatenate([pair_part, value_part], axis=-1) * D ** (-0.5)
    return joined.astype(jnp.bfloat16)


def steps_of(stream_key, dims, split, least, high):
    def one(position, parts):
        draws = jax.random.uniform(jax.random.fold_in(jax.random.fold_in(stream_key, 6), position), (parts,), jnp.float32, least / len(split), high / len(split))
        return jnp.repeat(jnp.exp(draws), dims[position] // parts).reshape((-1,) + (1,) * (len(dims) - position - 1))

    gain = one(*split[0])
    for cut in split[1:]:
        gain = gain * one(*cut)
    return gain


def length_profile(amount, total, bound, lean):
    portions = [(1 << 20) // math.isqrt(grade ** lean) + 1 for grade in range(2, amount + 1)]
    spare, holding = total - bound - (amount - 1), [1] * (amount - 1)
    while spare > 0:
        free = [i for i in range(amount - 1) if holding[i] < bound]
        mass, budget = sum([portions[i] for i in free]), spare
        for i in free:
            addition = min(bound - holding[i], max(1, budget * portions[i] // mass), spare)
            holding[i] = holding[i] + addition
            spare = spare - addition
    return np.array([bound] + holding)


def ragged_sizes(key, amount, total, bound, slope):
    if amount == 2:
        one = jax.random.randint(key, (), max(1, total - bound), min(bound, total - 1) + 1)
        return jnp.stack([one, total - one])
    lengths = jnp.asarray(length_profile(amount, total, bound, slope), jnp.int32)
    pairs = (amount - 1) // 2
    giver, taker = lengths[1:1 + 2 * pairs:2], lengths[2:2 + 2 * pairs:2]
    margin = jnp.minimum(giver - 1, bound - taker)
    passed = jax.random.randint(jax.random.fold_in(key, 1), (pairs,), 0, 1 << 20) % (margin + 1)
    lengths = lengths.at[1:1 + 2 * pairs:2].set(giver - passed).at[2:2 + 2 * pairs:2].set(taker + passed)
    return lengths[jax.random.permutation(jax.random.fold_in(key, 2), amount)]


def normal_values(key, shape, spread, reach, shards=(), kind=jnp.bfloat16):
    level = steps_of(key, shape, shards, -0.22, 0.18) if shards else 1.0
    array = jax.random.normal(key, shape, jnp.float32) * spread * level
    return jnp.minimum(jnp.maximum(array, -reach), reach).astype(kind)


def setup_inputs(seed: int = 0) -> dict:
    splits = jax.random.split(jax.random.key(seed), 9)
    responses = normal_values(splits[0], (BINS, SRC_ROWS, D), 1.0, 6.0, ((0, 32), (1, 16)))
    kl_terms = normal_values(splits[1], (BINS, RESP, LMAX), 0.5, 3.0, ((0, 32),))
    norm_gain = jnp.clip(1.0 + 0.1 * jax.random.normal(splits[2], (D,), jnp.float32), 0.5, 1.5)
    w_qkv = draw_w_qkv(jax.random.fold_in(splits[8], 71), 0)
    readout = normal_values(splits[4], (HEADS, HD), HD ** -0.5, 0.5, ((0, 16),))
    slot_bin = draw_slot_bin(jax.random.fold_in(splits[8], 71), 0)
    entry_source = draw_entry_source(jax.random.fold_in(splits[8], 71), 0)
    bin_segments = jax.vmap(lambda own: jnp.searchsorted(jnp.cumsum(ragged_sizes(own, RESP, BIN_DEV, CAP, 1)), jnp.arange(BIN_DEV), side="right"))(jax.random.split(splits[7], BINS)).reshape((BINS, BIN_DEV)).astype(jnp.int32)
    return {"responses": responses, "kl_terms": kl_terms, "norm_gain": norm_gain, "w_qkv": w_qkv, "readout": readout, "slot_bin": slot_bin, "entry_source": entry_source, "bin_segments": bin_segments}


epsilon = 1e-06
beta_weight = 0.05
score_scale = 1.0 / 12.0
soft_cap = 50.0
rope_base = 10000.0

def rms_scaled(features, gain_vec):
    widened = features.astype(jnp.float32)
    mean_square = lax.optimization_barrier(jnp.mean(widened * widened, axis=-1, keepdims=True))
    return (widened * lax.rsqrt(mean_square + epsilon) * gain_vec).astype(jnp.bfloat16)

def rotate(heads_block, positions):
    halfway = heads_block.shape[-1] // 2
    frequency = rope_base ** (-2.0 * jnp.arange(halfway, dtype=jnp.float32) / heads_block.shape[-1])
    angles = positions.astype(jnp.float32)[:, None] * frequency[None, :]
    cosine = jnp.cos(angles)[:, None, :]
    sine_part = jnp.sin(angles)[:, None, :]
    widened = heads_block.astype(jnp.float32)
    first_half = widened[..., :halfway]
    second = widened[..., halfway:]
    joined = jnp.concatenate([first_half * cosine - second * sine_part, second * cosine + first_half * sine_part], axis=-1)
    return joined.astype(jnp.bfloat16)

def attend(queries, keys_rot, values, allowed):
    logits = jnp.einsum('qd,kd->qk', queries.astype(jnp.float32), keys_rot.astype(jnp.float32)) * score_scale
    capped = soft_cap * jnp.tanh(logits / soft_cap)
    expo = jnp.where(allowed, jnp.exp(capped), 0.0)
    probs = (expo / lax.optimization_barrier(jnp.sum(expo, axis=-1, keepdims=True))).astype(jnp.bfloat16)
    return jnp.dot(probs, values, preferred_element_type=jnp.float32).astype(jnp.bfloat16)

def reference(responses, kl_terms, norm_gain, w_qkv, readout, slot_bin, entry_source, bin_segments):
    weights = w_qkv.reshape(D, HEADS * 3 * HD)
    piece_ids = jnp.arange(N_TENSOR, dtype=jnp.int32)

    def one_bin(bin_index):
        segments = bin_segments[bin_index]
        seg_onehot = (segments[:, None] == jnp.arange(RESP, dtype=jnp.int32)[None, :]).astype(jnp.int32)
        piece_rows = lax.optimization_barrier(jnp.sum(seg_onehot, axis=0))
        offsets = jnp.cumsum(piece_rows) - piece_rows
        within = jnp.arange(BIN_DEV, dtype=jnp.int32) - offsets[segments]
        sources = entry_source[bin_index][segments]
        source_rows = piece_ids[:, None] * (RESP * CAP) + segments[None, :] * CAP + within[None, :]
        packed = responses[sources[None, :], source_rows].reshape(BIN_TOK, D)
        normed = rms_scaled(packed, norm_gain)
        raw_heads = jnp.dot(normed, weights, preferred_element_type=jnp.float32).astype(jnp.bfloat16)
        raw_heads = raw_heads.reshape(BIN_TOK, HEADS, 3, HD)
        positions = (piece_ids[:, None] * piece_rows[segments][None, :] + within[None, :]).reshape(-1)
        all_segments = jnp.tile(segments, N_TENSOR)
        queries = rotate(raw_heads[:, :, 0], positions)
        keys_rot = rotate(raw_heads[:, :, 1], positions)
        values = raw_heads[:, :, 2]
        allowed = (all_segments[:, None] == all_segments[None, :]) & (positions[None, :] <= positions[:, None])

        def one_head(operands):
            return attend(operands[0], operands[1], operands[2], allowed)
        outputs = lax.map(one_head, (jnp.transpose(queries, (1, 0, 2)), jnp.transpose(keys_rot, (1, 0, 2)), jnp.transpose(values, (1, 0, 2))))
        head_rows = jnp.transpose(outputs, (1, 0, 2))
        last_rows = (N_TENSOR - 1) * BIN_DEV + offsets + piece_rows - 1
        picked = head_rows[last_rows].astype(jnp.float32)
        reward_part = lax.optimization_barrier(jnp.sum(picked * readout.astype(jnp.float32)[None, :, :], axis=(1, 2)))
        chosen = slot_bin == bin_index
        entry_kl = lax.optimization_barrier(jnp.sum(jnp.where(chosen[:, :, None], kl_terms.astype(jnp.float32), 0.0), axis=0))
        tokens = jnp.arange(LMAX, dtype=jnp.int32)
        live_tokens = tokens[None, :] < (piece_rows * N_TENSOR)[:, None]
        penalty = lax.optimization_barrier(jnp.sum(jnp.where(live_tokens, entry_kl, 0.0), axis=1))
        return (head_rows.reshape(BIN_TOK, HEADS * HD), reward_part - beta_weight * penalty)
    head_outputs, scores = lax.map(one_bin, jnp.arange(BINS, dtype=jnp.int32))
    return (head_outputs, scores)
```

```python
import jax
import jax.numpy as jnp
import numpy as np
from jax import lax
from jax.experimental import pallas as pl
from jax.experimental.pallas import tpu as pltpu
from jax.sharding import PartitionSpec as P

D = 4608
HALF_D = D // 2
HD = 128
RESP = 8
CAP = 10
BIN_DEV = 64
LMAX = 160
PIECES = 16
NZ = 16
CHUNK = 16
CHUNKS = 5
ROWS = PIECES * CHUNK
ROWS_DEV = 80

epsilon = 1e-06
beta_weight = 0.05
score_scale = 1.0 / 12.0
soft_cap = 50.0
rope_base = 10000.0

F32 = jnp.float32
BF16 = jnp.bfloat16
I32 = jnp.int32


def iota(shape, dim):
    return lax.broadcasted_iota(I32, shape, dim)


def slot_of(row):
    slot = jnp.zeros_like(row)
    for j in range(1, RESP):
        slot = slot + jnp.where(row >= CAP * j, 1, 0)
    return slot


def per_slot(slot, counts):
    out = jnp.zeros(slot.shape, I32)
    for j in range(RESP):
        out = jnp.where(slot == j, counts[j], out)
    return out


def kernel(
    resp, kl, gain, freq, w_hbm, readout, slot_bin, entry_source, bin_segments,
    out, scores,
    gath, w, meta, cos_t, sin_t, qs, ks, vs, os, zb, sel0, sel1, ob, rx, ry, sc,
    w_sem, r1, r2, ag_send, meta_send, meta_recv, p1_send, p1_recv, sib_send, sib_recv,
    p2_send, p2_recv, rw_send, rw_recv,
):
    d = lax.axis_index("dp")
    t = lax.axis_index("tensor")
    z, core = d // 2, d % 2
    y, x = t // 4, t % 4
    a = (1 - core) * x + core * y
    b = (1 - core) * y + core * x

    def piece(i, j):
        i, j = (a + i) % 4, (b + j) % 4
        return (1 - core) * (j * 4 + i) + core * (i * 4 + j)

    def in_z(target):
        return {"dp": target * 2 + core}

    sibling = {"dp": z * 2 + (1 - core)}

    def remote(src, dst, send, recv, device):
        return pltpu.make_async_remote_copy(
            src_ref=src, dst_ref=dst, send_sem=send, recv_sem=recv,
            device_id=device, device_id_type=pl.DeviceIdType.MESH,
        )

    def drain(ref, sem):
        pltpu.make_async_copy(ref, ref, sem).wait()

    w_copy = pltpu.make_async_copy(w_hbm, w, w_sem)
    w_copy.start()
    barrier = pltpu.get_barrier_semaphore()

    def greet(device):
        pl.semaphore_signal(barrier, inc=1, device_id=device, device_id_type=pl.DeviceIdType.MESH)

    for i in range(1, 4):
        greet({"tensor": piece(i, 0)})
        greet({"tensor": piece(0, i)})
    greet(sibling)

    def greet_z(i, carry):
        greet(in_z((z + i) % NZ))
        return carry

    lax.fori_loop(1, NZ, greet_z, 0)

    lane = iota((1, HD), 1)
    meta[core, z] = jnp.full((8, HD), 99, I32)
    meta[core, z, 0:1, 0:BIN_DEV] = bin_segments[...]
    meta[core, z, 1:2, 0:RESP] = entry_source[...]

    for c in range(CHUNKS):
        rows = resp[CHUNK * c:CHUNK * (c + 1), :].astype(F32)
        mean_square = jnp.sum(rows * rows, axis=-1, keepdims=True) * (1.0 / D)
        normed = rows * lax.rsqrt(mean_square + epsilon) * gain[...]
        gath[c, t] = normed.astype(BF16)

    pl.semaphore_wait(barrier, 6 + 1 + NZ - 1)

    lo, hi = pl.ds(0, HALF_D), pl.ds(HALF_D, HALF_D)
    up_a, down_a = {"tensor": piece(1, 0)}, {"tensor": piece(-1, 0)}
    up_b, down_b = {"tensor": piece(0, 1)}, {"tensor": piece(0, -1)}
    order = (0, -1, 1, 2)

    def full(c, p, sem, device):
        return remote(gath.at[c, p], gath.at[c, p], ag_send.at[c], sem, device)

    def half(c, p, cols, sem, device):
        view = gath.at[c, p, :, cols]
        return remote(view, view, ag_send.at[c], sem, device)

    def second_sends(c, i):
        p = piece(order[i], 0)
        full(c, p, r2.at[c, i, 0], up_b).start()
        full(c, p, r2.at[c, i, 1], down_b).start()

    def first_ring(c):
        if c == 0:
            second_sends(c, 0)
        full(c, piece(-1, 0), r1.at[c, 0], up_a).wait_recv()
        half(c, piece(-1, 0), lo, r1.at[c, 2], up_a).start()
        if c > 0:
            second_sends(c, 0)
        second_sends(c, 1)
        full(c, piece(1, 0), r1.at[c, 1], down_a).wait_recv()
        half(c, piece(1, 0), hi, r1.at[c, 3], down_a).start()
        second_sends(c, 2)
        half(c, piece(2, 0), lo, r1.at[c, 2], up_a).wait_recv()
        half(c, piece(2, 0), hi, r1.at[c, 3], down_a).wait_recv()
        second_sends(c, 3)

    def second_ring(c):
        for i in range(4):
            below, above = piece(order[i], -1), piece(order[i], 1)
            full(c, below, r2.at[c, i, 0], up_b).wait_recv()
            half(c, below, lo, r2.at[c, i, 2], up_b).start()
            full(c, above, r2.at[c, i, 1], down_b).wait_recv()
            half(c, above, hi, r2.at[c, i, 3], down_b).start()

    def second_end(c):
        for i in range(4):
            opposite = piece(order[i], 2)
            half(c, opposite, lo, r2.at[c, i, 2], up_b).wait_recv()
            half(c, opposite, hi, r2.at[c, i, 3], down_b).wait_recv()

    for c in range(CHUNKS):
        full(c, t, r1.at[c, 0], up_a).start()
        full(c, t, r1.at[c, 1], down_a).start()

    def send_z(ref_of, dst, send, recv):
        def body(i, carry):
            target = (z + i) % NZ
            remote(ref_of(target), dst, send, recv, in_z(target)).start()
            return carry

        lax.fori_loop(1, NZ, body, 0)

    send_z(lambda target: meta.at[core, z], meta.at[core, z], meta_send.at[0], meta_recv.at[0])

    first_ring(0)

    drain(meta.at[core, pl.ds(0, NZ - 1)], meta_recv.at[0])
    meta_pass = remote(meta.at[core], meta.at[core], meta_send.at[1], meta_recv.at[1], sibling)
    meta_pass.start()
    remote(meta.at[1 - core], meta.at[1 - core], meta_send.at[1], meta_recv.at[1], sibling).wait_recv()

    every = meta[...].reshape(2 * NZ, 8, HD)
    tile_row = iota((2 * NZ, 8, HD), 1)
    tile_id = iota((2 * NZ, 8, HD), 0)
    tile_bin = (tile_id % NZ) * 2 + tile_id // NZ
    is_segment = tile_row == 0
    own_bins = jnp.full((1, HD), -1, I32)
    for j in range(RESP):
        own_bins = jnp.where(lane == j, slot_bin[0:1, j:j + 1], own_bins)
    counts = []
    for j in range(RESP):
        hit = is_segment & (every == j) & (tile_bin == slot_bin[0:1, j:j + 1].reshape(1, 1, 1))
        counts.append(jnp.sum(jnp.where(hit, 1.0, 0.0)).astype(I32))

    last_row = jnp.full((1, HD), -1, I32)
    penalty = jnp.zeros((1, HD), F32)
    token = iota((1, LMAX), 1)
    for j in range(RESP):
        last_row = jnp.where(lane == j, CAP * j + counts[j] - 1, last_row)
        live = jnp.where(token < counts[j] * PIECES, kl[j:j + 1, :].astype(F32), 0.0)
        penalty = jnp.where(lane == j, jnp.sum(live, axis=1, keepdims=True), penalty)

    def rope_tables(c, carry):
        index = iota((ROWS, HD), 0)
        row = CHUNK * c + index % CHUNK
        slot = slot_of(row)
        position = (index // CHUNK) * per_slot(slot, counts) + row - CAP * slot
        angle = position.astype(F32) * freq[...]
        cos_t[c] = jnp.cos(angle)
        sine = jnp.sin(angle)
        sin_t[c] = jnp.where(iota((ROWS, HD), 1) < HD // 2, -sine, sine)
        return carry

    lax.fori_loop(0, CHUNKS, rope_tables, 0)

    def pick_rows(i, carry):
        tile = meta[core, i]
        seg_row = tile[0:1, :].astype(F32)
        src_row = tile[1:2, :].astype(F32)
        r_col = iota((BIN_DEV, HD), 0)
        l_row = iota((BIN_DEV, HD), 1)
        seg = jnp.sum(jnp.where(r_col == l_row, seg_row, 0.0), axis=1, keepdims=True)
        offset = jnp.sum(jnp.where(seg_row < seg, 1.0, 0.0), axis=1, keepdims=True)
        source = jnp.sum(jnp.where(l_row.astype(F32) == seg, src_row, 0.0), axis=1, keepdims=True)
        source = source.astype(I32)
        row = CAP * seg.astype(I32) + r_col[:, 0:1] - offset.astype(I32)
        base = ((source & 1) * NZ + (source >> 1)) * 32
        late = jnp.where(row < 60, NZ * 64 + row - 32, NZ * 128 + row - 48)
        column = base + jnp.where(row < 32, row, late)
        top = iota((32, 64 * NZ * 2), 1) == column[0:32]
        sel0[i] = jnp.where(top, 1.0, 0.0).astype(BF16)
        low = iota((32, 96 * NZ * 2), 1) == column[32:64]
        sel1[i] = jnp.where(low, 1.0, 0.0).astype(BF16)
        return carry

    lax.fori_loop(0, NZ, pick_rows, 0)

    def project(c):
        raw = jnp.dot(gath[c].reshape(ROWS, D), w[...], preferred_element_type=F32).astype(BF16)

        def rotate(part):
            part = part.astype(F32)
            turned = part * cos_t[c] + pltpu.roll(part, HD // 2, 1) * sin_t[c]
            return turned.astype(BF16)

        qs[c] = rotate(raw[:, 0:HD])
        ks[c] = rotate(raw[:, HD:2 * HD])
        vs[c] = raw[:, 2 * HD:3 * HD]

    def attend(cq, first, count):
        index = iota((ROWS, 1), 0)
        row = CHUNK * cq + index % CHUNK
        slot = slot_of(row)
        low = slot * LMAX
        high = low + (index // CHUNK) * CAP + row - CAP * slot
        es = []
        for ck in range(first, first + count):
            kidx = iota((1, ROWS), 1)
            krow = CHUNK * ck + kidx % CHUNK
            kslot = slot_of(krow)
            within = krow - CAP * kslot
            code = kslot * LMAX + (kidx // CHUNK) * CAP + within
            code = jnp.where(within < per_slot(kslot, counts), code, RESP * LMAX)
            s = lax.dot_general(qs[cq], ks[ck], (((1,), (1,)), ((), ())), preferred_element_type=F32)
            capped = soft_cap * jnp.tanh(s * (score_scale / soft_cap))
            allowed = (code >= low) & (code <= high)
            es.append(jnp.where(allowed, jnp.exp(capped), 0.0))
        total = sum(jnp.sum(e, axis=-1, keepdims=True) for e in es)
        inverse = 1.0 / jnp.maximum(total, 1e-30)
        result = jnp.zeros((ROWS, HD), F32)
        for ck, e in zip(range(first, first + count), es):
            probs = (e * inverse).astype(BF16)
            result = result + jnp.dot(probs, vs[ck], preferred_element_type=F32)
        return result.astype(BF16).reshape(PIECES, CHUNK, HD)

    def to_pieces(k):
        send_z(lambda target: os.at[k, target], zb.at[k, core, z], p1_send.at[k], p1_recv.at[k])
        zb[k, core, z] = os[k, z]

    def share(k):
        drain(zb.at[k, core, pl.ds(0, NZ - 1)], p1_recv.at[k])
        remote(zb.at[k, core], zb.at[k, core], sib_send.at[k], sib_recv.at[k], sibling).start()

    def shared(k):
        remote(zb.at[k, 1 - core], zb.at[k, 1 - core], sib_send.at[k], sib_recv.at[k], sibling).wait_recv()

    def to_bins(h, sel):
        depth = sel.shape[-1]
        src = zb[0:depth // (NZ * 64)].reshape(depth, HD)
        rows = jnp.dot(sel[...].reshape(NZ * 32, depth), src, preferred_element_type=F32)
        ob[h] = rows.astype(BF16).reshape(NZ, 32, HD)
        place = pl.ds(pl.multiple_of(z * BIN_DEV + 32 * h, 32), 32)
        send_z(lambda target: ob.at[h, target], out.at[place], p2_send.at[h], p2_recv.at[h])
        own = pltpu.make_async_copy(ob.at[h, z], out.at[place], p2_send.at[2 + h])
        own.start()
        return own

    w_copy.wait()

    first_ring(1)
    second_ring(0)
    first_ring(2)
    second_ring(1)
    second_end(0)
    project(0)
    first_ring(3)
    second_ring(2)
    second_end(1)
    project(1)
    os[0, :, 0:CHUNK, :] = attend(0, 0, 2)
    first_ring(4)
    second_ring(3)
    second_end(2)
    project(2)
    os[0, :, CHUNK:32, :] = attend(1, 0, 3)
    to_pieces(0)
    second_ring(4)
    second_end(3)
    project(3)
    os[1, :, 0:CHUNK, :] = attend(2, 1, 3)
    os[1, :, CHUNK:32, :] = attend(3, 2, 2)
    to_pieces(1)
    share(0)
    share(1)
    shared(0)
    shared(1)
    own0 = to_bins(0, sel0)
    second_end(4)
    project(4)
    os[2, :, 0:CHUNK, :] = attend(3, 3, 2)
    os[2, :, CHUNK:32, :] = attend(4, 3, 2)
    to_pieces(2)

    reward = jnp.zeros((1, HD), F32)
    gains = readout[...].astype(F32)
    for k, (start, least, most) in enumerate(((0, 0, 32), (32, 32, 60), (48, 60, 80))):
        value = jnp.sum(os[k, PIECES - 1].astype(F32) * gains, axis=1, keepdims=True)
        row = start + iota((32, 1), 0)
        use = (row == last_row) & (row >= least) & (row < most)
        reward = reward + jnp.sum(jnp.where(use, value, 0.0), axis=0, keepdims=True)

    def sum_ring(buf, index, own, k, device_of):
        buf[index] = jnp.broadcast_to(own, (8, HD))
        for i in range(1, 4):
            remote(buf.at[index], buf.at[index], rw_send.at[k], rw_recv.at[k], device_of(i)).start()
        drain(buf.at[pl.ds(0, 3)], rw_recv.at[k])
        return (buf[0] + buf[1] + buf[2] + buf[3])[0:1, :]

    reward = sum_ring(rx, x, reward, 0, lambda i: {"tensor": y * 4 + (x + i) % 4})
    reward = sum_ring(ry, y, reward, 1, lambda i: {"tensor": ((y + i) % 4) * 4 + x})
    sc[core, z] = jnp.broadcast_to(reward - beta_weight * penalty, (8, HD))
    send_z(lambda target: sc.at[core, z], sc.at[core, z], rw_send.at[2], rw_recv.at[2])

    share(2)
    shared(2)
    own1 = to_bins(1, sel1)

    drain(sc.at[core, pl.ds(0, NZ - 1)], rw_recv.at[2])
    sc_pass = remote(sc.at[core], sc.at[core], rw_send.at[3], rw_recv.at[3], sibling)
    sc_pass.start()
    remote(sc.at[1 - core], sc.at[1 - core], rw_send.at[3], rw_recv.at[3], sibling).wait_recv()
    all_scores = sc[...].reshape(2 * NZ, 8, HD)
    sources = jnp.full((1, HD), -1, I32)
    for j in range(RESP):
        sources = jnp.where(lane == j, entry_source[0:1, j:j + 1], sources)
    mine = (tile_bin == sources.reshape(1, 1, HD)) & is_segment
    picked = jnp.sum(jnp.where(mine, all_scores, 0.0), axis=0)
    scores[...] = jnp.sum(picked, axis=0, keepdims=True)[:, 0:RESP]

    own0.wait()
    own1.wait()
    for h in range(2):
        drain(ob.at[h, pl.ds(0, NZ - 1)], p2_recv.at[h])
        drain(ob.at[h, pl.ds(0, NZ - 1)], p2_send.at[h])
    for k in range(3):
        drain(os.at[k, pl.ds(0, NZ - 1)], p1_send.at[k])
        drain(zb.at[k, core], sib_send.at[k])
    for c in range(CHUNKS):
        drain(gath.at[c, pl.ds(0, 15)], ag_send.at[c])
    drain(meta.at[core, pl.ds(0, NZ - 1)], meta_send.at[0])
    drain(meta.at[core], meta_send.at[1])
    drain(rx.at[pl.ds(0, 3)], rw_send.at[0])
    drain(ry.at[pl.ds(0, 3)], rw_send.at[1])
    drain(sc.at[core, pl.ds(0, NZ - 1)], rw_send.at[2])
    drain(sc.at[core], rw_send.at[3])


def body(responses, kl_terms, norm_gain, w_qkv, readout, slot_bin, entry_source, bin_segments):
    steps = np.arange(HD // 2, dtype=np.float32)
    frequency = (np.float32(rope_base) ** (-2.0 * steps / HD)).astype(np.float32)
    freq = jnp.asarray(np.concatenate([frequency, frequency])[None, :])
    vmem = pl.BlockSpec(memory_space=pltpu.VMEM)
    hbm = pl.BlockSpec(memory_space=pl.ANY)
    dma = pltpu.SemaphoreType.DMA
    out, scores = pl.pallas_call(
        kernel,
        out_shape=(
            jax.ShapeDtypeStruct((PIECES * BIN_DEV, HD), BF16),
            jax.ShapeDtypeStruct((1, RESP), F32),
        ),
        in_specs=[vmem, vmem, vmem, vmem, hbm, vmem, vmem, vmem, vmem],
        out_specs=(hbm, vmem),
        scratch_shapes=[
            pltpu.VMEM((CHUNKS, PIECES, CHUNK, D), BF16),
            pltpu.VMEM((D, 3 * HD), BF16),
            pltpu.VMEM((2, NZ, 8, HD), I32),
            pltpu.VMEM((CHUNKS, ROWS, HD), F32),
            pltpu.VMEM((CHUNKS, ROWS, HD), F32),
            pltpu.VMEM((CHUNKS, ROWS, HD), BF16),
            pltpu.VMEM((CHUNKS, ROWS, HD), BF16),
            pltpu.VMEM((CHUNKS, ROWS, HD), BF16),
            pltpu.VMEM((3, PIECES, 32, HD), BF16),
            pltpu.VMEM((3, 2, NZ, 32, HD), BF16),
            pltpu.VMEM((NZ, 32, 64 * NZ * 2), BF16),
            pltpu.VMEM((NZ, 32, 96 * NZ * 2), BF16),
            pltpu.VMEM((2, NZ, 32, HD), BF16),
            pltpu.VMEM((4, 8, HD), F32),
            pltpu.VMEM((4, 8, HD), F32),
            pltpu.VMEM((2, NZ, 8, HD), F32),
            dma,
            dma((CHUNKS, 4)),
            dma((CHUNKS, 4, 4)),
            dma((CHUNKS,)),
            dma((2,)),
            dma((2,)),
            dma((3,)),
            dma((3,)),
            dma((3,)),
            dma((3,)),
            dma((4,)),
            dma((2,)),
            dma((4,)),
            dma((4,)),
        ],
        compiler_params=pltpu.CompilerParams(
            collective_id=0, has_side_effects=True, vmem_limit_bytes=56 * 1024 * 1024
        ),
    )(
        responses[0], kl_terms[0], norm_gain[None, :], freq, w_qkv.reshape(D, 3 * HD),
        readout, slot_bin, entry_source, bin_segments,
    )
    return out[None], scores


def solution(mesh):
    placed = (
        P("dp", "tensor", None),
        P("dp", None, None),
        P(),
        P(None, "tensor", None),
        P("tensor", None),
        P("dp", None),
        P("dp", None),
        P("dp", None),
    )
    return jax.shard_map(
        body,
        mesh=mesh,
        in_specs=placed,
        out_specs=(P("dp", None, "tensor"), P("dp", None)),
        check_vma=False,
    )
```

```python
import jax
import jax.numpy as jnp
import numpy as np
from jax import lax
from jax.experimental import pallas as pl
from jax.experimental.pallas import tpu as pltpu
from jax.sharding import PartitionSpec as P

D = 4608
HD = 128
RESP = 8
CAP = 10
BIN_DEV = 64
LMAX = 160
PIECES = 16
NZ = 16
CHUNK = 16
ROWS = PIECES * CHUNK
LATE = 5
FOLD = D // 4
FOLD_LO = 640
MAIN = 256
EXTRA = 128

epsilon = 1e-06
beta_weight = 0.05
score_scale = 1.0 / 12.0
soft_cap = 50.0
rope_base = 10000.0

F32 = jnp.float32
BF16 = jnp.bfloat16
I32 = jnp.int32


def iota(shape, dim):
    return lax.broadcasted_iota(I32, shape, dim)


def slot_of(row):
    slot = jnp.zeros_like(row)
    for j in range(1, RESP):
        slot = slot + jnp.where(row >= CAP * j, 1, 0)
    return slot


def per_slot(slot, counts):
    out = jnp.zeros(slot.shape, I32)
    for j in range(RESP):
        out = jnp.where(slot == j, counts[j], out)
    return out


def kernel(
    resp, kl, gain, freq, w_hbm, readout, slot_bin, entry_source, bin_segments,
    out, scores,
    ge, gx, gl, nb, w, meta, cos_t, sin_t, low_t, high_t, code_t, qs, ks, vs,
    ib, ibx, io, iox, seli, os, zb, sel, ob, fo, rx, sc,
    w_sem, r1, r2, ag_send, meta_send, meta_recv, i_send, i_recv, ix_send, ix_recv,
    p1_send, p1_recv, sib_send, sib_recv, p2_send, p2_recv, rw_send, rw_recv, own_sem,
):
    d = lax.axis_index("dp")
    t = lax.axis_index("tensor")
    z, core = d // 2, d % 2
    y, x = t // 4, t % 4
    a = (1 - core) * x + core * y
    b = (1 - core) * y + core * x

    def piece(i, j):
        i, j = (a + i) % 4, (b + j) % 4
        return (1 - core) * (j * 4 + i) + core * (i * 4 + j)

    def in_z(target):
        return {"dp": target * 2 + core}

    sibling = {"dp": z * 2 + (1 - core)}

    def remote(src, dst, send, recv, device):
        return pltpu.make_async_remote_copy(
            src_ref=src, dst_ref=dst, send_sem=send, recv_sem=recv,
            device_id=device, device_id_type=pl.DeviceIdType.MESH,
        )

    def drain(ref, sem):
        pltpu.make_async_copy(ref, ref, sem).wait()

    def over_z(step):
        def body(i, carry):
            step((z + i) % NZ)
            return carry

        lax.fori_loop(1, NZ, body, 0)

    w_copy = pltpu.make_async_copy(w_hbm, w, w_sem)
    w_copy.start()
    barrier = pltpu.get_barrier_semaphore()

    def greet(device):
        pl.semaphore_signal(barrier, inc=1, device_id=device, device_id_type=pl.DeviceIdType.MESH)

    over_z(lambda target: greet(in_z(target)))
    for i in range(1, 4):
        greet({"tensor": piece(i, 0)})
        greet({"tensor": piece(0, i)})
    greet(sibling)

    lane = iota((1, HD), 1)
    meta[core, z] = jnp.full((8, HD), 99, I32)
    meta[core, z, 0:1, 0:BIN_DEV] = bin_segments[...]
    meta[core, z, 1:2, 0:RESP] = entry_source[...]

    gains = gain[...]
    gains = jnp.concatenate([gains[i:i + 1, :] for i in range(D // HD)], axis=1)
    for c in range(5):
        rows = resp[CHUNK * c:CHUNK * (c + 1), :].astype(F32)
        mean_square = jnp.sum(rows * rows, axis=-1, keepdims=True) * (1.0 / D)
        normed = (rows * lax.rsqrt(mean_square + epsilon) * gains).astype(BF16)
        if c < 3:
            ge[c, t] = normed
        else:
            nb[CHUNK * (c - 3):CHUNK * (c - 2), :] = normed
        if c == 3:
            wide = normed.astype(F32)
            block = iota((CHUNK, FOLD), 0) // 4
            folded = wide[:, 0:FOLD]
            for q in range(1, 4):
                part = pltpu.roll(wide[:, FOLD * q:FOLD * (q + 1)], 4 * q, 0)
                folded = jnp.where(block == q, part, folded)
            gx[t] = folded.astype(BF16)

    pl.semaphore_wait(barrier, 6 + 1 + NZ - 1)

    up_a, down_a = {"tensor": piece(1, 0)}, {"tensor": piece(-1, 0)}
    up_b, down_b = {"tensor": piece(0, 1)}, {"tensor": piece(0, -1)}
    order = (0, -1, 1, 2)

    def view(c, p, part=None):
        if c == 3:
            cut = {None: pl.ds(0, FOLD), 0: pl.ds(0, FOLD_LO), 1: pl.ds(FOLD_LO, FOLD - FOLD_LO)}[part]
            return gx.at[p, :, cut]
        cut = {None: pl.ds(0, D), 0: pl.ds(0, D // 2), 1: pl.ds(D // 2, D // 2)}[part]
        if c < 3:
            return ge.at[c, p, :, cut]
        return gl.at[p, pl.ds(CHUNK * (c - 4), CHUNK), cut]

    def full(c, p, sem, device):
        return remote(view(c, p), view(c, p), ag_send.at[c], sem, device)

    def half(c, p, part, sem, device):
        return remote(view(c, p, part), view(c, p, part), ag_send.at[c], sem, device)

    def second_sends(c, i):
        p = piece(order[i], 0)
        full(c, p, r2.at[c, i, 0], up_b).start()
        full(c, p, r2.at[c, i, 1], down_b).start()

    def first_sends(c):
        full(c, t, r1.at[c, 0], up_a).start()
        full(c, t, r1.at[c, 1], down_a).start()

    def first_ring(c):
        full(c, piece(-1, 0), r1.at[c, 0], up_a).wait_recv()
        half(c, piece(-1, 0), 0, r1.at[c, 2], up_a).start()
        second_sends(c, 1)
        full(c, piece(1, 0), r1.at[c, 1], down_a).wait_recv()
        half(c, piece(1, 0), 1, r1.at[c, 3], down_a).start()
        second_sends(c, 2)
        half(c, piece(2, 0), 0, r1.at[c, 2], up_a).wait_recv()
        half(c, piece(2, 0), 1, r1.at[c, 3], down_a).wait_recv()
        second_sends(c, 3)

    def second_ring(c):
        for i in range(4):
            below, above = piece(order[i], -1), piece(order[i], 1)
            full(c, below, r2.at[c, i, 0], up_b).wait_recv()
            half(c, below, 0, r2.at[c, i, 2], up_b).start()
            full(c, above, r2.at[c, i, 1], down_b).wait_recv()
            half(c, above, 1, r2.at[c, i, 3], down_b).start()

    def second_end(c):
        for i in range(4):
            opposite = piece(order[i], 2)
            half(c, opposite, 0, r2.at[c, i, 2], up_b).wait_recv()
            half(c, opposite, 1, r2.at[c, i, 3], down_b).wait_recv()

    def main_cols(target):
        return pl.ds(pl.multiple_of(target * MAIN, MAIN), MAIN)

    def extra_cols(target):
        return pl.ds(pl.multiple_of(NZ * MAIN + (target // 4) * EXTRA, EXTRA), EXTRA)

    def spread(target):
        remote(nb.at[:, main_cols(target)], ib.at[core, z], i_send.at[0], i_recv.at[0], in_z(target)).start()

        @pl.when(target % 4 == 0)
        def _():
            remote(nb.at[:, extra_cols(target)], ibx.at[core, z], ix_send.at[0], ix_recv.at[0], in_z(target)).start()

    def collect(target):
        remote(io.at[target], gl.at[t, :, main_cols(z)], i_send.at[1], i_recv.at[1], in_z(target)).start()

        @pl.when(z % 4 == 0)
        def _():
            remote(iox.at[target], gl.at[t, :, extra_cols(z)], ix_send.at[1], ix_recv.at[1], in_z(target)).start()

    first_sends(0)
    second_sends(0, 0)
    first_sends(1)
    over_z(spread)
    first_sends(2)
    first_sends(3)
    over_z(lambda target: remote(
        meta.at[core, z], meta.at[core, z], meta_send.at[0], meta_recv.at[0], in_z(target)).start())
    ib[core, z] = nb[:, main_cols(z)]

    @pl.when(z % 4 == 0)
    def _():
        ibx[core, z] = nb[:, extra_cols(z)]

    first_ring(0)
    second_sends(1, 0)
    first_ring(1)

    drain(meta.at[core, pl.ds(0, NZ - 1)], meta_recv.at[0])
    meta_pass = remote(meta.at[core], meta.at[core], meta_send.at[1], meta_recv.at[1], sibling)
    meta_pass.start()
    second_ring(0)

    def bin_rows(tile, start, size):
        seg_row = tile[0:1, :].astype(F32)
        src_row = tile[1:2, :].astype(F32)
        r_col = start + iota((size, HD), 0)
        l_row = iota((size, HD), 1)
        seg = jnp.sum(jnp.where(r_col == l_row, seg_row, 0.0), axis=1, keepdims=True)
        number = jnp.sum(jnp.where(seg_row == seg, 1.0, 0.0), axis=1, keepdims=True)
        offset = jnp.sum(jnp.where(seg_row < seg, 1.0, 0.0), axis=1, keepdims=True)
        source = jnp.sum(jnp.where(l_row.astype(F32) == seg, src_row, 0.0), axis=1, keepdims=True)
        source = source.astype(I32)
        within = r_col[:, 0:1].astype(F32) - offset
        return seg, number, within, (source & 1) * NZ + (source >> 1)

    def pick_late(i, carry):
        seg, _, within, place = bin_rows(meta[core, i], 32, 32)
        row = CAP * seg.astype(I32) + within.astype(I32) - 48
        column = jnp.where(seg >= LATE, place * 32 + row, -1)
        seli[i] = jnp.where(iota((32, 2 * NZ * 32), 1) == column, 1.0, 0.0).astype(BF16)
        return carry

    lax.fori_loop(0, NZ, pick_late, 0)

    drain(ib.at[core, pl.ds(0, NZ - 1)], i_recv.at[0])
    ib_pass = remote(ib.at[core], ib.at[core], sib_send.at[2], sib_recv.at[2], sibling)
    ib_pass.start()

    @pl.when(z % 4 == 0)
    def _():
        drain(ibx.at[core, pl.ds(0, NZ - 1)], ix_recv.at[0])
        remote(ibx.at[core], ibx.at[core], sib_send.at[3], sib_recv.at[3], sibling).start()

    second_sends(2, 0)
    first_ring(2)
    second_ring(1)

    remote(ib.at[1 - core], ib.at[1 - core], sib_send.at[2], sib_recv.at[2], sibling).wait_recv()
    picks = seli[...].reshape(NZ * 32, 2 * NZ * 32)
    rows = jnp.dot(picks, ib[...].reshape(2 * NZ * 32, MAIN), preferred_element_type=F32)
    io[...] = rows.astype(BF16).reshape(NZ, 32, MAIN)

    @pl.when(z % 4 == 0)
    def _():
        remote(ibx.at[1 - core], ibx.at[1 - core], sib_send.at[3], sib_recv.at[3], sibling).wait_recv()
        rows = jnp.dot(picks, ibx[...].reshape(2 * NZ * 32, EXTRA), preferred_element_type=F32)
        iox[...] = rows.astype(BF16).reshape(NZ, 32, EXTRA)

    over_z(collect)
    gl[t, :, main_cols(z)] = io[z]

    @pl.when(z % 4 == 0)
    def _():
        gl[t, :, extra_cols(z)] = iox[z]

    remote(meta.at[1 - core], meta.at[1 - core], meta_send.at[1], meta_recv.at[1], sibling).wait_recv()

    every = meta[...].reshape(2 * NZ, 8, HD)
    tile_row = iota((2 * NZ, 8, HD), 1)
    tile_id = iota((2 * NZ, 8, HD), 0)
    tile_bin = (tile_id % NZ) * 2 + tile_id // NZ
    is_segment = tile_row == 0
    counts = []
    for j in range(RESP):
        hit = is_segment & (every == j) & (tile_bin == slot_bin[0:1, j:j + 1].reshape(1, 1, 1))
        counts.append(jnp.sum(jnp.where(hit, 1.0, 0.0)).astype(I32))

    def rope_tables(c, carry):
        index = iota((ROWS, HD), 0)
        row = CHUNK * c + index % CHUNK
        slot = slot_of(row)
        position = (index // CHUNK) * per_slot(slot, counts) + row - CAP * slot
        angle = position.astype(F32) * freq[...]
        cos_t[c] = jnp.cos(angle)
        sine = jnp.sin(angle)
        sin_t[c] = jnp.where(iota((ROWS, HD), 1) < HD // 2, -sine, sine)
        return carry

    def rotated(raw, c):
        def rotate(part):
            part = part.astype(F32)
            turned = part * cos_t[c] + pltpu.roll(part, HD // 2, 1) * sin_t[c]
            return turned.astype(BF16)

        qs[c] = rotate(raw[:, 0:HD])
        ks[c] = rotate(raw[:, HD:2 * HD])
        vs[c] = raw[:, 2 * HD:3 * HD]

    def project(c):
        rows = ge[c] if c < 3 else gl[:, CHUNK * (c - 4):CHUNK * (c - 3), :]
        raw = jnp.dot(rows.reshape(ROWS, D), w[...], preferred_element_type=F32)
        rotated(raw.astype(BF16), c)

    def project_folded():
        rows = gx[...].reshape(ROWS, FOLD)
        raw = jnp.dot(rows, w[0:FOLD, :], preferred_element_type=F32)
        for q in range(1, 4):
            part = jnp.dot(rows, w[FOLD * q:FOLD * (q + 1), :], preferred_element_type=F32)
            raw = raw + pltpu.roll(part, ROWS - 4 * q, 0)
        rotated(raw.astype(BF16), 3)

    def softmax_values(q, low, high, keys):
        es = []
        for ck, code in keys:
            s = lax.dot_general(q, ks[ck], (((1,), (1,)), ((), ())), preferred_element_type=F32)
            capped = soft_cap * jnp.tanh(s * (score_scale / soft_cap))
            allowed = (code >= low) & (code <= high)
            es.append(jnp.where(allowed, jnp.exp(capped), 0.0))
        total = sum(jnp.sum(e, axis=-1, keepdims=True) for e in es)
        inverse = 1.0 / jnp.maximum(total, 1e-30)
        result = jnp.zeros((q.shape[0], HD), F32)
        for (ck, _), e in zip(keys, es):
            result = result + jnp.dot((e * inverse).astype(BF16), vs[ck], preferred_element_type=F32)
        return result.astype(BF16)

    def attend(cq, first, count):
        index = iota((ROWS, 1), 0)
        row = CHUNK * cq + index % CHUNK
        slot = slot_of(row)
        low = slot * LMAX
        high = low + (index // CHUNK) * CAP + row - CAP * slot
        keys = []
        for ck in range(first, first + count):
            kidx = iota((1, ROWS), 1)
            krow = CHUNK * ck + kidx % CHUNK
            kslot = slot_of(krow)
            within = krow - CAP * kslot
            code = kslot * LMAX + (kidx // CHUNK) * CAP + within
            live = (within < per_slot(kslot, counts)) & (kslot < LATE)
            keys.append((ck, jnp.where(live, code, 2 * RESP * LMAX)))
        return softmax_values(qs[cq], low, high, keys).reshape(PIECES, CHUNK, HD)

    def to_pieces(k):
        over_z(lambda target: remote(
            os.at[k, target], zb.at[k, core, z], p1_send.at[k], p1_recv.at[k], in_z(target)).start())
        zb[k, core, z] = os[k, z]

    def share(k):
        drain(zb.at[k, core, pl.ds(0, NZ - 1)], p1_recv.at[k])
        remote(zb.at[k, core], zb.at[k, core], sib_send.at[k], sib_recv.at[k], sibling).start()

    def shared(k):
        remote(zb.at[k, 1 - core], zb.at[k, 1 - core], sib_send.at[k], sib_recv.at[k], sibling).wait_recv()

    def pick_early(i, carry):
        seg, _, within, place = bin_rows(meta[core, i], 0, BIN_DEV)
        row = CAP * seg.astype(I32) + within.astype(I32)
        column = place * 32 + jnp.where(row < 32, row, 2 * NZ * 32 + row - 32)
        column = jnp.where(seg < LATE, column, -1)
        sel[i] = jnp.where(iota((BIN_DEV, 2 * NZ * 64), 1) == column, 1.0, 0.0).astype(BF16)
        return carry

    def late_tables():
        seg, number, within, _ = bin_rows(meta[core, z], 32, 32)
        for c in range(2):
            def spread_rows(col):
                col = col[CHUNK * c:CHUNK * (c + 1)].reshape(1, CHUNK, 1)
                return jnp.broadcast_to(col, (PIECES, CHUNK, HD)).reshape(ROWS, HD)

            slot = spread_rows(seg)
            position = (iota((ROWS, HD), 0) // CHUNK).astype(F32) * spread_rows(number) + spread_rows(within)
            angle = position * freq[...]
            cos_t[4 + c] = jnp.cos(angle)
            sine = jnp.sin(angle)
            sin_t[4 + c] = jnp.where(iota((ROWS, HD), 1) < HD // 2, -sine, sine)
            live = slot >= LATE
            low_t[c] = jnp.where(live, slot * LMAX, 4.0 * RESP * LMAX)
            high_t[c] = jnp.where(live, slot * LMAX + position, -1.0)
            code = jnp.where(live, slot * LMAX + position, 2.0 * RESP * LMAX)
            code_t[c] = jnp.transpose(code)[0:8, :]

    def late_keys():
        return [(4, code_t[0, 0:1, :]), (5, code_t[1, 0:1, :])]

    lax.fori_loop(0, 4, rope_tables, 0)
    w_copy.wait()
    second_end(0)
    project(0)
    first_ring(3)
    second_sends(3, 0)
    second_ring(2)
    second_end(1)
    project(1)
    os[0, :, 0:CHUNK, :] = attend(0, 0, 2)
    second_ring(3)
    lax.fori_loop(0, NZ, pick_early, 0)
    second_end(3)
    project_folded()
    second_end(2)
    project(2)
    os[1, :, 0:CHUNK, :] = attend(2, 1, 3)
    os[1, :, CHUNK:32, :] = attend(3, 2, 2)
    to_pieces(1)

    drain(io.at[pl.ds(0, NZ - 1)], i_recv.at[1])

    @pl.when(z % 4 == 0)
    def _():
        drain(iox.at[pl.ds(0, 3)], ix_recv.at[1])

    @pl.when(z % 4 != 0)
    def _():
        drain(iox.at[pl.ds(0, 4)], ix_recv.at[1])

    first_sends(4)
    second_sends(4, 0)
    first_sends(5)
    os[0, :, CHUNK:32, :] = attend(1, 0, 3)
    to_pieces(0)
    first_ring(4)

    weights = readout[...].astype(F32)
    last_row = jnp.full((1, HD), -1, I32)
    penalty = jnp.zeros((1, HD), F32)
    token = iota((1, LMAX), 1)
    for j in range(RESP):
        if j < LATE:
            last_row = jnp.where(lane == j, CAP * j + counts[j] - 1, last_row)
        live = jnp.where(token < counts[j] * PIECES, kl[j:j + 1, :].astype(F32), 0.0)
        penalty = jnp.where(lane == j, jnp.sum(live, axis=1, keepdims=True), penalty)

    def reward_of(rows, row, wanted):
        value = jnp.sum(rows.astype(F32) * weights, axis=1, keepdims=True)
        return jnp.sum(jnp.where(row == wanted, value, 0.0), axis=0, keepdims=True)

    reward = jnp.zeros((1, HD), F32)
    for k in range(2):
        reward = reward + reward_of(os[k, PIECES - 1], 32 * k + iota((32, 1), 0), last_row)

    def ring_x(i):
        return {"tensor": y * 4 + (x + i) % 4}

    def ring_y(i):
        return {"tensor": ((y + i) % 4) * 4 + x}

    def sum_start(buf, k, index, own, device_of):
        buf[k, index] = jnp.broadcast_to(own, (8, HD))
        for i in range(1, 4):
            remote(buf.at[k, index], buf.at[k, index], rw_send.at[k], rw_recv.at[k], device_of(i)).start()

    def sum_end(buf, k):
        drain(buf.at[k, pl.ds(0, 3)], rw_recv.at[k])
        return (buf[k, 0] + buf[k, 1] + buf[k, 2] + buf[k, 3])[0:1, :]

    sum_start(rx, 0, x, reward, ring_x)
    late_tables()
    second_ring(4)
    second_sends(5, 0)
    first_ring(5)
    reward = sum_end(rx, 0)
    sum_start(rx, 1, y, reward, ring_y)
    share(1)
    share(0)
    reward = sum_end(rx, 1)
    sc[core, z] = jnp.broadcast_to(reward - beta_weight * penalty, (8, HD))
    over_z(lambda target: remote(
        sc.at[core, z], sc.at[core, z], rw_send.at[4], rw_recv.at[4], in_z(target)).start())
    shared(1)
    shared(0)
    src = zb[...].reshape(2 * NZ * 64, HD)
    rows = jnp.dot(sel[...].reshape(NZ * BIN_DEV, 2 * NZ * 64), src, preferred_element_type=F32)
    ob[...] = rows.astype(BF16).reshape(NZ, BIN_DEV, HD)
    over_z(lambda target: remote(
        ob.at[target], fo.at[z], p2_send, p2_recv, in_z(target)).start())
    fo[z] = ob[z]

    second_ring(5)
    second_end(4)
    project(4)
    drain(sc.at[core, pl.ds(0, NZ - 1)], rw_recv.at[4])
    sc_pass = remote(sc.at[core], sc.at[core], rw_send.at[5], rw_recv.at[5], sibling)
    sc_pass.start()

    seg_row = meta[core, z, 0:1, :]
    late_last = jnp.full((1, HD), -1, I32)
    for j in range(LATE, RESP):
        upto = jnp.sum(jnp.where(seg_row <= j, 1.0, 0.0), axis=1, keepdims=True).astype(I32)
        late_last = jnp.where(lane == j, upto - 33, late_last)

    second_end(5)
    project(5)
    tail = pl.ds(ROWS - CHUNK, CHUNK)
    q_last = jnp.concatenate([qs[4, tail, :], qs[5, tail, :]], axis=0)
    low = jnp.concatenate([low_t[0, tail, 0:1], low_t[1, tail, 0:1]], axis=0)
    high = jnp.concatenate([high_t[0, tail, 0:1], high_t[1, tail, 0:1]], axis=0)
    last_rows = softmax_values(q_last, low, high, late_keys())
    sum_start(rx, 2, x, reward_of(last_rows, iota((32, 1), 0), late_last), ring_x)
    late = []
    late.append(softmax_values(qs[4], low_t[0, :, 0:1], high_t[0, :, 0:1], late_keys()))
    reward = sum_end(rx, 2)
    sum_start(rx, 3, y, reward, ring_y)
    late.append(softmax_values(qs[5], low_t[1, :, 0:1], high_t[1, :, 0:1], late_keys()))

    drain(ob.at[pl.ds(0, NZ - 1)], p2_recv)
    for c in range(2):
        rows = pl.ds(32 + CHUNK * c, CHUNK)
        mine = late[c].reshape(PIECES, CHUNK, HD).astype(F32)
        fo[:, rows, :] = (fo[:, rows, :].astype(F32) + mine).astype(BF16)
    out_copy = pltpu.make_async_copy(fo, out, own_sem)
    out_copy.start()

    remote(sc.at[1 - core], sc.at[1 - core], rw_send.at[5], rw_recv.at[5], sibling).wait_recv()
    all_scores = sc[...].reshape(2 * NZ, 8, HD)
    sources = jnp.full((1, HD), -1, I32)
    for j in range(RESP):
        sources = jnp.where(lane == j, entry_source[0:1, j:j + 1], sources)
    mine = (tile_bin == sources.reshape(1, 1, HD)) & is_segment
    picked = jnp.sum(jnp.where(mine, all_scores, 0.0), axis=0)
    picked = jnp.sum(picked, axis=0, keepdims=True)

    for c in range(6):
        if c < 3:
            sent = ge.at[c, pl.ds(0, 15)]
        elif c == 3:
            sent = gx.at[pl.ds(0, 15)]
        else:
            sent = gl.at[pl.ds(0, 15), pl.ds(CHUNK * (c - 4), CHUNK)]
        drain(sent, ag_send.at[c])
    drain(io.at[pl.ds(0, NZ - 1)], i_send.at[0])
    drain(io.at[pl.ds(0, NZ - 1)], i_send.at[1])

    @pl.when(z % 4 == 0)
    def _():
        drain(iox.at[pl.ds(0, 3)], ix_send.at[0])
        drain(iox.at[pl.ds(0, NZ - 1)], ix_send.at[1])
        drain(ibx.at[core], sib_send.at[3])

    @pl.when(z % 4 != 0)
    def _():
        drain(iox.at[pl.ds(0, 4)], ix_send.at[0])

    for k in range(2):
        drain(os.at[k, pl.ds(0, NZ - 1)], p1_send.at[k])
        drain(zb.at[k, core], sib_send.at[k])
    drain(ib.at[core], sib_send.at[2])
    drain(ob.at[pl.ds(0, NZ - 1)], p2_send)
    drain(meta.at[core, pl.ds(0, NZ - 1)], meta_send.at[0])
    drain(meta.at[core], meta_send.at[1])
    for k in range(3):
        drain(rx.at[k, pl.ds(0, 3)], rw_send.at[k])
    drain(sc.at[core, pl.ds(0, NZ - 1)], rw_send.at[4])
    drain(sc.at[core], rw_send.at[5])
    reward = sum_end(rx, 3)
    scores[...] = (picked + reward)[:, 0:RESP]
    drain(rx.at[3, pl.ds(0, 3)], rw_send.at[3])
    out_copy.wait()


def body(responses, kl_terms, norm_gain, w_qkv, readout, slot_bin, entry_source, bin_segments):
    steps = np.arange(HD // 2, dtype=np.float32)
    frequency = (np.float32(rope_base) ** (-2.0 * steps / HD)).astype(np.float32)
    freq = jnp.asarray(np.concatenate([frequency, frequency])[None, :])
    vmem = pl.BlockSpec(memory_space=pltpu.VMEM)
    hbm = pl.BlockSpec(memory_space=pl.ANY)
    dma = pltpu.SemaphoreType.DMA
    out, scores = pl.pallas_call(
        kernel,
        out_shape=(
            jax.ShapeDtypeStruct((PIECES, BIN_DEV, HD), BF16),
            jax.ShapeDtypeStruct((1, RESP), F32),
        ),
        in_specs=[vmem, vmem, vmem, vmem, hbm, vmem, vmem, vmem, vmem],
        out_specs=(hbm, vmem),
        scratch_shapes=[
            pltpu.VMEM((3, PIECES, CHUNK, D), BF16),
            pltpu.VMEM((PIECES, CHUNK, FOLD), BF16),
            pltpu.VMEM((PIECES, 2 * CHUNK, D), BF16),
            pltpu.VMEM((2 * CHUNK, D), BF16),
            pltpu.VMEM((D, 3 * HD), BF16),
            pltpu.VMEM((2, NZ, 8, HD), I32),
            pltpu.VMEM((6, ROWS, HD), F32),
            pltpu.VMEM((6, ROWS, HD), F32),
            pltpu.VMEM((2, ROWS, HD), F32),
            pltpu.VMEM((2, ROWS, HD), F32),
            pltpu.VMEM((2, 8, ROWS), F32),
            pltpu.VMEM((6, ROWS, HD), BF16),
            pltpu.VMEM((6, ROWS, HD), BF16),
            pltpu.VMEM((6, ROWS, HD), BF16),
            pltpu.VMEM((2, NZ, 32, MAIN), BF16),
            pltpu.VMEM((2, NZ, 32, EXTRA), BF16),
            pltpu.VMEM((NZ, 32, MAIN), BF16),
            pltpu.VMEM((NZ, 32, EXTRA), BF16),
            pltpu.VMEM((NZ, 32, 2 * NZ * 32), BF16),
            pltpu.VMEM((2, PIECES, 32, HD), BF16),
            pltpu.VMEM((2, 2, NZ, 32, HD), BF16),
            pltpu.VMEM((NZ, BIN_DEV, 2 * NZ * 64), BF16),
            pltpu.VMEM((NZ, BIN_DEV, HD), BF16),
            pltpu.VMEM((PIECES, BIN_DEV, HD), BF16),
            pltpu.VMEM((4, 4, 8, HD), F32),
            pltpu.VMEM((2, NZ, 8, HD), F32),
            dma,
            dma((6, 4)),
            dma((6, 4, 4)),
            dma((6,)),
            dma((2,)),
            dma((2,)),
            dma((2,)),
            dma((2,)),
            dma((2,)),
            dma((2,)),
            dma((2,)),
            dma((2,)),
            dma((4,)),
            dma((4,)),
            dma,
            dma,
            dma((6,)),
            dma((6,)),
            dma,
        ],
        compiler_params=pltpu.CompilerParams(
            collective_id=0, has_side_effects=True, vmem_limit_bytes=58 * 1024 * 1024
        ),
    )(
        responses[0], kl_terms[0], norm_gain.reshape(D // HD, HD), freq, w_qkv.reshape(D, 3 * HD),
        readout, slot_bin, entry_source, bin_segments,
    )
    return out.reshape(1, PIECES * BIN_DEV, HD), scores


def solution(mesh):
    placed = (
        P("dp", "tensor", None),
        P("dp", None, None),
        P(),
        P(None, "tensor", None),
        P("tensor", None),
        P("dp", None),
        P("dp", None),
        P("dp", None),
    )
    return jax.shard_map(
        body,
        mesh=mesh,
        in_specs=placed,
        out_specs=(P("dp", None, "tensor"), P("dp", None)),
        check_vma=False,
    )
```

```python
import jax
import jax.numpy as jnp
import numpy as np
from jax import lax
from jax.experimental import pallas as pl
from jax.experimental.pallas import tpu as pltpu
from jax.sharding import PartitionSpec as P

D = 4608
HD = 128
RESP = 8
CAP = 10
BIN_DEV = 64
LMAX = 160
PIECES = 16
NZ = 16
CHUNK = 16
ROWS = PIECES * CHUNK
LATE = 5
FOLD = D // 4
FOLD_LO = 640
MAIN = 256
EXTRA = 128

epsilon = 1e-06
beta_weight = 0.05
score_scale = 1.0 / 12.0
soft_cap = 50.0
rope_base = 10000.0

F32 = jnp.float32
BF16 = jnp.bfloat16
I32 = jnp.int32


def iota(shape, dim):
    return lax.broadcasted_iota(I32, shape, dim)


def slot_of(row):
    slot = jnp.zeros_like(row)
    for j in range(1, RESP):
        slot = slot + jnp.where(row >= CAP * j, 1, 0)
    return slot


def per_slot(slot, counts):
    out = jnp.zeros(slot.shape, I32)
    for j in range(RESP):
        out = jnp.where(slot == j, counts[j], out)
    return out


def kernel(
    resp, kl, gain, freq, w_hbm, readout, slot_bin, entry_source, bin_segments,
    out, scores,
    ge, gx, gl, nb, w, meta, cos_t, sin_t, low_t, high_t, code_t, qs, ks, vs,
    ib, ibx, io, iox, seli, os, zb, sel, ob, fo, rx, sc,
    w_sem, r1, r2, ag_send, meta_send, meta_recv, i_send, i_recv, ix_send, ix_recv,
    p1_send, p1_recv, sib_send, sib_recv, p2_send, p2_recv, rw_send, rw_recv, own_sem,
):
    d = lax.axis_index("dp")
    t = lax.axis_index("tensor")
    z, core = d // 2, d % 2
    y, x = t // 4, t % 4
    a = (1 - core) * x + core * y
    b = (1 - core) * y + core * x

    def piece(i, j):
        i, j = (a + i) % 4, (b + j) % 4
        return (1 - core) * (j * 4 + i) + core * (i * 4 + j)

    def in_z(target):
        return {"dp": target * 2 + core}

    sibling = {"dp": z * 2 + (1 - core)}

    def remote(src, dst, send, recv, device):
        return pltpu.make_async_remote_copy(
            src_ref=src, dst_ref=dst, send_sem=send, recv_sem=recv,
            device_id=device, device_id_type=pl.DeviceIdType.MESH,
        )

    def drain(ref, sem):
        pltpu.make_async_copy(ref, ref, sem).wait()

    def over_z(step):
        def body(i, carry):
            step((z + i) % NZ)
            return carry

        lax.fori_loop(1, NZ, body, 0)

    def over_plane(step):
        def body(i, carry):
            step((t + i) % PIECES)
            return carry

        lax.fori_loop(1, PIECES, body, 0)

    w_copy = pltpu.make_async_copy(w_hbm, w, w_sem)
    w_copy.start()
    barrier = pltpu.get_barrier_semaphore()

    def greet(device):
        pl.semaphore_signal(barrier, inc=1, device_id=device, device_id_type=pl.DeviceIdType.MESH)

    over_z(lambda target: greet(in_z(target)))
    over_plane(lambda target: greet({"tensor": target}))
    greet(sibling)

    lane = iota((1, HD), 1)
    meta[core, z] = jnp.full((8, HD), 99, I32)
    meta[core, z, 0:1, 0:BIN_DEV] = bin_segments[...]
    meta[core, z, 1:2, 0:RESP] = entry_source[...]

    gains = gain[...]
    gains = jnp.concatenate([gains[i:i + 1, :] for i in range(D // HD)], axis=1)
    for c in range(5):
        rows = resp[CHUNK * c:CHUNK * (c + 1), :].astype(F32)
        mean_square = jnp.sum(rows * rows, axis=-1, keepdims=True) * (1.0 / D)
        normed = (rows * lax.rsqrt(mean_square + epsilon) * gains).astype(BF16)
        if c < 3:
            ge[c, t] = normed
        else:
            nb[CHUNK * (c - 3):CHUNK * (c - 2), :] = normed
        if c == 3:
            wide = normed.astype(F32)
            block = iota((CHUNK, FOLD), 0) // 4
            folded = wide[:, 0:FOLD]
            for q in range(1, 4):
                part = pltpu.roll(wide[:, FOLD * q:FOLD * (q + 1)], 4 * q, 0)
                folded = jnp.where(block == q, part, folded)
            gx[t] = folded.astype(BF16)

    pl.semaphore_wait(barrier, PIECES - 1 + 1 + NZ - 1)

    up_a, down_a = {"tensor": piece(1, 0)}, {"tensor": piece(-1, 0)}
    up_b, down_b = {"tensor": piece(0, 1)}, {"tensor": piece(0, -1)}
    order = (0, -1, 1, 2)

    def view(c, p, part=None):
        if c == 3:
            cut = {None: pl.ds(0, FOLD), 0: pl.ds(0, FOLD_LO), 1: pl.ds(FOLD_LO, FOLD - FOLD_LO)}[part]
            return gx.at[p, :, cut]
        cut = {None: pl.ds(0, D), 0: pl.ds(0, D // 2), 1: pl.ds(D // 2, D // 2)}[part]
        if c < 3:
            return ge.at[c, p, :, cut]
        return gl.at[p, pl.ds(CHUNK * (c - 4), CHUNK), cut]

    def full(c, p, sem, device):
        return remote(view(c, p), view(c, p), ag_send.at[c], sem, device)

    def half(c, p, part, sem, device):
        return remote(view(c, p, part), view(c, p, part), ag_send.at[c], sem, device)

    def second_sends(c, i):
        p = piece(order[i], 0)
        full(c, p, r2.at[c, i, 0], up_b).start()
        full(c, p, r2.at[c, i, 1], down_b).start()

    def first_sends(c):
        full(c, t, r1.at[c, 0], up_a).start()
        full(c, t, r1.at[c, 1], down_a).start()

    def first_ring(c):
        full(c, piece(-1, 0), r1.at[c, 0], up_a).wait_recv()
        half(c, piece(-1, 0), 0, r1.at[c, 2], up_a).start()
        second_sends(c, 1)
        full(c, piece(1, 0), r1.at[c, 1], down_a).wait_recv()
        half(c, piece(1, 0), 1, r1.at[c, 3], down_a).start()
        second_sends(c, 2)
        half(c, piece(2, 0), 0, r1.at[c, 2], up_a).wait_recv()
        half(c, piece(2, 0), 1, r1.at[c, 3], down_a).wait_recv()
        second_sends(c, 3)

    def second_ring(c):
        for i in range(4):
            below, above = piece(order[i], -1), piece(order[i], 1)
            full(c, below, r2.at[c, i, 0], up_b).wait_recv()
            half(c, below, 0, r2.at[c, i, 2], up_b).start()
            full(c, above, r2.at[c, i, 1], down_b).wait_recv()
            half(c, above, 1, r2.at[c, i, 3], down_b).start()

    def second_end(c):
        for i in range(4):
            opposite = piece(order[i], 2)
            half(c, opposite, 0, r2.at[c, i, 2], up_b).wait_recv()
            half(c, opposite, 1, r2.at[c, i, 3], down_b).wait_recv()

    def main_cols(target):
        return pl.ds(pl.multiple_of(target * MAIN, MAIN), MAIN)

    def extra_cols(target):
        return pl.ds(pl.multiple_of(NZ * MAIN + (target // 4) * EXTRA, EXTRA), EXTRA)

    def spread(target):
        remote(nb.at[:, main_cols(target)], ib.at[core, z], i_send.at[0], i_recv.at[0], in_z(target)).start()

        @pl.when(target % 4 == 0)
        def _():
            remote(nb.at[:, extra_cols(target)], ibx.at[core, z], ix_send.at[0], ix_recv.at[0], in_z(target)).start()

    def collect(target):
        remote(io.at[target], gl.at[t, :, main_cols(z)], i_send.at[1], i_recv.at[1], in_z(target)).start()

        @pl.when(z % 4 == 0)
        def _():
            remote(iox.at[target], gl.at[t, :, extra_cols(z)], ix_send.at[1], ix_recv.at[1], in_z(target)).start()

    first_sends(3)
    second_sends(3, 0)
    first_sends(0)
    second_sends(0, 0)
    over_z(spread)
    first_sends(1)
    second_sends(1, 0)
    over_z(lambda target: remote(
        meta.at[core, z], meta.at[core, z], meta_send.at[0], meta_recv.at[0], in_z(target)).start())
    first_sends(2)
    ib[core, z] = nb[:, main_cols(z)]

    @pl.when(z % 4 == 0)
    def _():
        ibx[core, z] = nb[:, extra_cols(z)]

    first_ring(3)
    first_ring(0)
    second_sends(2, 0)
    second_ring(3)
    first_ring(1)

    drain(meta.at[core, pl.ds(0, NZ - 1)], meta_recv.at[0])
    meta_pass = remote(meta.at[core], meta.at[core], meta_send.at[1], meta_recv.at[1], sibling)
    meta_pass.start()

    def bin_rows(tile, start, size):
        seg_row = tile[0:1, :].astype(F32)
        src_row = tile[1:2, :].astype(F32)
        r_col = start + iota((size, HD), 0)
        l_row = iota((size, HD), 1)
        seg = jnp.sum(jnp.where(r_col == l_row, seg_row, 0.0), axis=1, keepdims=True)
        number = jnp.sum(jnp.where(seg_row == seg, 1.0, 0.0), axis=1, keepdims=True)
        offset = jnp.sum(jnp.where(seg_row < seg, 1.0, 0.0), axis=1, keepdims=True)
        source = jnp.sum(jnp.where(l_row.astype(F32) == seg, src_row, 0.0), axis=1, keepdims=True)
        source = source.astype(I32)
        within = r_col[:, 0:1].astype(F32) - offset
        return seg, number, within, (source & 1) * NZ + (source >> 1)

    def pick_late(i, carry):
        seg, _, within, place = bin_rows(meta[core, i], 32, 32)
        row = CAP * seg.astype(I32) + within.astype(I32) - 48
        column = jnp.where(seg >= LATE, place * 32 + row, -1)
        seli[i] = jnp.where(iota((32, 2 * NZ * 32), 1) == column, 1.0, 0.0).astype(BF16)
        return carry

    def late_tables():
        seg, number, within, _ = bin_rows(meta[core, z], 32, 32)
        for c in range(2):
            def spread_rows(col):
                col = col[CHUNK * c:CHUNK * (c + 1)].reshape(1, CHUNK, 1)
                return jnp.broadcast_to(col, (PIECES, CHUNK, HD)).reshape(ROWS, HD)

            slot = spread_rows(seg)
            position = (iota((ROWS, HD), 0) // CHUNK).astype(F32) * spread_rows(number) + spread_rows(within)
            angle = position * freq[...]
            cos_t[4 + c] = jnp.cos(angle)
            sine = jnp.sin(angle)
            sin_t[4 + c] = jnp.where(iota((ROWS, HD), 1) < HD // 2, -sine, sine)
            live = slot >= LATE
            low_t[c] = jnp.where(live, slot * LMAX, 4.0 * RESP * LMAX)
            high_t[c] = jnp.where(live, slot * LMAX + position, -1.0)
            code = jnp.where(live, slot * LMAX + position, 2.0 * RESP * LMAX)
            code_t[c] = jnp.transpose(code)[0:8, :]

    late_tables()
    def pick_early(i, carry):
        seg, _, within, place = bin_rows(meta[core, i], 0, BIN_DEV)
        row = CAP * seg.astype(I32) + within.astype(I32)
        column = place * 32 + jnp.where(row < 30, row, 2 * NZ * 32 + jnp.where(row < 32, row, row - 32))
        column = jnp.where(seg < LATE, column, -1)
        sel[i] = jnp.where(iota((BIN_DEV, 2 * NZ * 64), 1) == column, 1.0, 0.0).astype(BF16)
        return carry

    lax.fori_loop(0, NZ, pick_late, 0)
    drain(ib.at[core, pl.ds(0, NZ - 1)], i_recv.at[0])
    ib_pass = remote(ib.at[core], ib.at[core], sib_send.at[2], sib_recv.at[2], sibling)
    ib_pass.start()

    @pl.when(z % 4 == 0)
    def _():
        drain(ibx.at[core, pl.ds(0, NZ - 1)], ix_recv.at[0])
        remote(ibx.at[core], ibx.at[core], sib_send.at[3], sib_recv.at[3], sibling).start()

    second_ring(0)
    remote(ib.at[1 - core], ib.at[1 - core], sib_send.at[2], sib_recv.at[2], sibling).wait_recv()
    picks = seli[...].reshape(NZ * 32, 2 * NZ * 32)
    rows = jnp.dot(picks, ib[...].reshape(2 * NZ * 32, MAIN), preferred_element_type=F32)
    io[...] = rows.astype(BF16).reshape(NZ, 32, MAIN)

    @pl.when(z % 4 == 0)
    def _():
        remote(ibx.at[1 - core], ibx.at[1 - core], sib_send.at[3], sib_recv.at[3], sibling).wait_recv()
        rows = jnp.dot(picks, ibx[...].reshape(2 * NZ * 32, EXTRA), preferred_element_type=F32)
        iox[...] = rows.astype(BF16).reshape(NZ, 32, EXTRA)

    over_z(collect)
    gl[t, :, main_cols(z)] = io[z]

    @pl.when(z % 4 == 0)
    def _():
        gl[t, :, extra_cols(z)] = iox[z]

    second_end(3)
    first_ring(2)
    second_ring(1)

    def rotated(raw, c):
        def rotate(part):
            part = part.astype(F32)
            turned = part * cos_t[c] + pltpu.roll(part, HD // 2, 1) * sin_t[c]
            return turned.astype(BF16)

        qs[c] = rotate(raw[:, 0:HD])
        ks[c] = rotate(raw[:, HD:2 * HD])
        vs[c] = raw[:, 2 * HD:3 * HD]

    def project(c):
        rows = ge[c] if c < 3 else gl[:, CHUNK * (c - 4):CHUNK * (c - 3), :]
        raw = jnp.dot(rows.reshape(ROWS, D), w[...], preferred_element_type=F32)
        rotated(raw.astype(BF16), c)

    def project_folded():
        rows = gx[...].reshape(ROWS, FOLD)
        raw = jnp.dot(rows, w[0:FOLD, :], preferred_element_type=F32)
        for q in range(1, 4):
            part = jnp.dot(rows, w[FOLD * q:FOLD * (q + 1), :], preferred_element_type=F32)
            raw = raw + pltpu.roll(part, ROWS - 4 * q, 0)
        rotated(raw.astype(BF16), 3)

    def softmax_values(q, low, high, keys):
        es = []
        for ck, code in keys:
            s = lax.dot_general(q, ks[ck], (((1,), (1,)), ((), ())), preferred_element_type=F32)
            capped = soft_cap * jnp.tanh(s * (score_scale / soft_cap))
            allowed = (code >= low) & (code <= high)
            es.append(jnp.where(allowed, jnp.exp(capped), 0.0))
        total = sum(jnp.sum(e, axis=-1, keepdims=True) for e in es)
        inverse = 1.0 / jnp.maximum(total, 1e-30)
        result = jnp.zeros((q.shape[0], HD), F32)
        for (ck, _), e in zip(keys, es):
            result = result + jnp.dot((e * inverse).astype(BF16), vs[ck], preferred_element_type=F32)
        return result.astype(BF16)

    def attend(cq, first, count):
        index = iota((ROWS, 1), 0)
        row = CHUNK * cq + index % CHUNK
        slot = slot_of(row)
        low = slot * LMAX
        high = low + (index // CHUNK) * CAP + row - CAP * slot
        keys = []
        for ck in range(first, first + count):
            kidx = iota((1, ROWS), 1)
            krow = CHUNK * ck + kidx % CHUNK
            kslot = slot_of(krow)
            within = krow - CAP * kslot
            code = kslot * LMAX + (kidx // CHUNK) * CAP + within
            live = (within < per_slot(kslot, counts)) & (kslot < LATE)
            keys.append((ck, jnp.where(live, code, 2 * RESP * LMAX)))
        return softmax_values(qs[cq], low, high, keys).reshape(PIECES, CHUNK, HD)

    def to_pieces(k):
        over_z(lambda target: remote(
            os.at[k, target], zb.at[k, core, z], p1_send.at[k], p1_recv.at[k], in_z(target)).start())
        zb[k, core, z] = os[k, z]

    def share(k):
        drain(zb.at[k, core, pl.ds(0, NZ - 1)], p1_recv.at[k])
        remote(zb.at[k, core], zb.at[k, core], sib_send.at[k], sib_recv.at[k], sibling).start()

    def shared(k):
        remote(zb.at[k, 1 - core], zb.at[k, 1 - core], sib_send.at[k], sib_recv.at[k], sibling).wait_recv()

    def late_keys():
        return [(4, code_t[0, 0:1, :]), (5, code_t[1, 0:1, :])]

    remote(meta.at[1 - core], meta.at[1 - core], meta_send.at[1], meta_recv.at[1], sibling).wait_recv()

    every = meta[...].reshape(2 * NZ, 8, HD)
    tile_row = iota((2 * NZ, 8, HD), 1)
    tile_id = iota((2 * NZ, 8, HD), 0)
    tile_bin = (tile_id % NZ) * 2 + tile_id // NZ
    is_segment = tile_row == 0
    counts = []
    for j in range(RESP):
        hit = is_segment & (every == j) & (tile_bin == slot_bin[0:1, j:j + 1].reshape(1, 1, 1))
        counts.append(jnp.sum(jnp.where(hit, 1.0, 0.0)).astype(I32))

    def rope_tables(c, carry):
        index = iota((ROWS, HD), 0)
        row = CHUNK * c + index % CHUNK
        slot = slot_of(row)
        position = (index // CHUNK) * per_slot(slot, counts) + row - CAP * slot
        angle = position.astype(F32) * freq[...]
        cos_t[c] = jnp.cos(angle)
        sine = jnp.sin(angle)
        sin_t[c] = jnp.where(iota((ROWS, HD), 1) < HD // 2, -sine, sine)
        return carry

    lax.fori_loop(0, 4, rope_tables, 0)
    w_copy.wait()
    project_folded()
    second_end(0)
    project(0)
    second_ring(2)

    lax.fori_loop(0, NZ, pick_early, 0)
    drain(io.at[pl.ds(0, NZ - 1)], i_recv.at[1])

    @pl.when(z % 4 == 0)
    def _():
        drain(iox.at[pl.ds(0, 3)], ix_recv.at[1])

    @pl.when(z % 4 != 0)
    def _():
        drain(iox.at[pl.ds(0, 4)], ix_recv.at[1])

    first_sends(4)
    second_sends(4, 0)
    first_sends(5)
    second_sends(5, 0)
    second_end(1)
    project(1)
    os[0, :, 0:CHUNK, :] = attend(0, 0, 2)
    os[0, :, CHUNK:32, :] = attend(1, 0, 2)
    to_pieces(0)
    second_end(2)
    project(2)
    os[1, :, 0:CHUNK, :] = attend(2, 1, 3)
    behind = iota((PIECES, CHUNK, HD), 1) >= CHUNK - 2
    os[1, :, CHUNK:32, :] = jnp.where(behind, attend(1, 1, 2), attend(3, 2, 2))
    to_pieces(1)
    first_ring(4)
    first_ring(5)
    share(0)
    second_ring(4)

    weights = readout[...].astype(F32)
    last_row = jnp.full((1, HD), -1, I32)
    penalty = jnp.zeros((1, HD), F32)
    token = iota((1, LMAX), 1)
    for j in range(RESP):
        if j < LATE:
            last_row = jnp.where(lane == j, CAP * j + counts[j] - 1, last_row)
        live = jnp.where(token < counts[j] * PIECES, kl[j:j + 1, :].astype(F32), 0.0)
        penalty = jnp.where(lane == j, jnp.sum(live, axis=1, keepdims=True), penalty)

    def reward_of(rows, row, wanted):
        value = jnp.sum(rows.astype(F32) * weights, axis=1, keepdims=True)
        return jnp.sum(jnp.where(row == wanted, value, 0.0), axis=0, keepdims=True)

    place = iota((32, 1), 0)
    reward = reward_of(os[0, PIECES - 1], jnp.where(place < 30, place, -5), last_row)
    reward = reward + reward_of(os[1, PIECES - 1], jnp.where(place < 30, 32 + place, place), last_row)

    reward = reward - jnp.where(t == 0, beta_weight, 0.0) * penalty
    sc[core, z] = jnp.broadcast_to(reward, (8, HD))
    over_z(lambda target: remote(
        sc.at[core, z], sc.at[core, z], rw_send.at[1], rw_recv.at[1], in_z(target)).start())
    share(1)
    shared(0)
    shared(1)
    src = zb[...].reshape(2 * NZ * 64, HD)
    rows = jnp.dot(sel[...].reshape(NZ * BIN_DEV, 2 * NZ * 64), src, preferred_element_type=F32)
    ob[...] = rows.astype(BF16).reshape(NZ, BIN_DEV, HD)
    over_z(lambda target: remote(
        ob.at[target], fo.at[z], p2_send, p2_recv, in_z(target)).start())
    fo[z] = ob[z]

    second_ring(5)
    drain(sc.at[core, pl.ds(0, NZ - 1)], rw_recv.at[1])
    sc_pass = remote(sc.at[core], sc.at[core], rw_send.at[2], rw_recv.at[2], sibling)
    sc_pass.start()

    seg_row = meta[core, z, 0:1, :]
    late_last = jnp.full((1, HD), -1, I32)
    for j in range(LATE, RESP):
        upto = jnp.sum(jnp.where(seg_row <= j, 1.0, 0.0), axis=1, keepdims=True).astype(I32)
        late_last = jnp.where(lane == j, upto - 33, late_last)

    second_end(4)
    project(4)
    remote(sc.at[1 - core], sc.at[1 - core], rw_send.at[2], rw_recv.at[2], sibling).wait_recv()
    all_scores = sc[...].reshape(2 * NZ, 8, HD)
    sources = jnp.full((1, HD), -1, I32)
    for j in range(RESP):
        sources = jnp.where(lane == j, entry_source[0:1, j:j + 1], sources)
    mine = (tile_bin == sources.reshape(1, 1, HD)) & is_segment
    picked = jnp.sum(jnp.where(mine, all_scores, 0.0), axis=0)
    picked = jnp.sum(picked, axis=0, keepdims=True)

    second_end(5)
    project(5)
    tail = pl.ds(ROWS - CHUNK, CHUNK)
    q_last = jnp.concatenate([qs[4, tail, :], qs[5, tail, :]], axis=0)
    low = jnp.concatenate([low_t[0, tail, 0:1], low_t[1, tail, 0:1]], axis=0)
    high = jnp.concatenate([high_t[0, tail, 0:1], high_t[1, tail, 0:1]], axis=0)
    last_rows = softmax_values(q_last, low, high, late_keys())
    rx[t] = jnp.broadcast_to(picked + reward_of(last_rows, place, late_last), (8, HD))
    over_plane(lambda target: remote(
        rx.at[t], rx.at[t], rw_send.at[0], rw_recv.at[0], {"tensor": target}).start())
    late = []
    late.append(softmax_values(qs[4], low_t[0, :, 0:1], high_t[0, :, 0:1], late_keys()))
    late.append(softmax_values(qs[5], low_t[1, :, 0:1], high_t[1, :, 0:1], late_keys()))

    drain(ob.at[pl.ds(0, NZ - 1)], p2_recv)
    for c in range(2):
        rows = pl.ds(32 + CHUNK * c, CHUNK)
        mine = late[c].reshape(PIECES, CHUNK, HD).astype(F32)
        fo[:, rows, :] = (fo[:, rows, :].astype(F32) + mine).astype(BF16)
    out_copy = pltpu.make_async_copy(fo, out, own_sem)
    out_copy.start()

    for c in range(6):
        if c < 3:
            sent = ge.at[c, pl.ds(0, 15)]
        elif c == 3:
            sent = gx.at[pl.ds(0, 15)]
        else:
            sent = gl.at[pl.ds(0, 15), pl.ds(CHUNK * (c - 4), CHUNK)]
        drain(sent, ag_send.at[c])
    drain(io.at[pl.ds(0, NZ - 1)], i_send.at[0])
    drain(io.at[pl.ds(0, NZ - 1)], i_send.at[1])

    @pl.when(z % 4 == 0)
    def _():
        drain(iox.at[pl.ds(0, 3)], ix_send.at[0])
        drain(iox.at[pl.ds(0, NZ - 1)], ix_send.at[1])
        drain(ibx.at[core], sib_send.at[3])

    @pl.when(z % 4 != 0)
    def _():
        drain(iox.at[pl.ds(0, 4)], ix_send.at[0])

    for k in range(2):
        drain(os.at[k, pl.ds(0, NZ - 1)], p1_send.at[k])
        drain(zb.at[k, core], sib_send.at[k])
    drain(ib.at[core], sib_send.at[2])
    drain(ob.at[pl.ds(0, NZ - 1)], p2_send)
    drain(meta.at[core, pl.ds(0, NZ - 1)], meta_send.at[0])
    drain(meta.at[core], meta_send.at[1])
    drain(sc.at[core, pl.ds(0, NZ - 1)], rw_send.at[1])
    drain(sc.at[core], rw_send.at[2])
    drain(rx.at[pl.ds(0, PIECES - 1)], rw_recv.at[0])
    scores[...] = jnp.sum(rx[...], axis=0)[0:1, 0:RESP]
    drain(rx.at[pl.ds(0, PIECES - 1)], rw_send.at[0])
    out_copy.wait()


def body(responses, kl_terms, norm_gain, w_qkv, readout, slot_bin, entry_source, bin_segments):
    steps = np.arange(HD // 2, dtype=np.float32)
    frequency = (np.float32(rope_base) ** (-2.0 * steps / HD)).astype(np.float32)
    freq = jnp.asarray(np.concatenate([frequency, frequency])[None, :])
    vmem = pl.BlockSpec(memory_space=pltpu.VMEM)
    hbm = pl.BlockSpec(memory_space=pl.ANY)
    dma = pltpu.SemaphoreType.DMA
    out, scores = pl.pallas_call(
        kernel,
        out_shape=(
            jax.ShapeDtypeStruct((PIECES, BIN_DEV, HD), BF16),
            jax.ShapeDtypeStruct((1, RESP), F32),
        ),
        in_specs=[vmem, vmem, vmem, vmem, hbm, vmem, vmem, vmem, vmem],
        out_specs=(hbm, vmem),
        scratch_shapes=[
            pltpu.VMEM((3, PIECES, CHUNK, D), BF16),
            pltpu.VMEM((PIECES, CHUNK, FOLD), BF16),
            pltpu.VMEM((PIECES, 2 * CHUNK, D), BF16),
            pltpu.VMEM((2 * CHUNK, D), BF16),
            pltpu.VMEM((D, 3 * HD), BF16),
            pltpu.VMEM((2, NZ, 8, HD), I32),
            pltpu.VMEM((6, ROWS, HD), F32),
            pltpu.VMEM((6, ROWS, HD), F32),
            pltpu.VMEM((2, ROWS, HD), F32),
            pltpu.VMEM((2, ROWS, HD), F32),
            pltpu.VMEM((2, 8, ROWS), F32),
            pltpu.VMEM((6, ROWS, HD), BF16),
            pltpu.VMEM((6, ROWS, HD), BF16),
            pltpu.VMEM((6, ROWS, HD), BF16),
            pltpu.VMEM((2, NZ, 32, MAIN), BF16),
            pltpu.VMEM((2, NZ, 32, EXTRA), BF16),
            pltpu.VMEM((NZ, 32, MAIN), BF16),
            pltpu.VMEM((NZ, 32, EXTRA), BF16),
            pltpu.VMEM((NZ, 32, 2 * NZ * 32), BF16),
            pltpu.VMEM((2, PIECES, 32, HD), BF16),
            pltpu.VMEM((2, 2, NZ, 32, HD), BF16),
            pltpu.VMEM((NZ, BIN_DEV, 2 * NZ * 64), BF16),
            pltpu.VMEM((NZ, BIN_DEV, HD), BF16),
            pltpu.VMEM((PIECES, BIN_DEV, HD), BF16),
            pltpu.VMEM((PIECES, 8, HD), F32),
            pltpu.VMEM((2, NZ, 8, HD), F32),
            dma,
            dma((6, 4)),
            dma((6, 4, 4)),
            dma((6,)),
            dma((2,)),
            dma((2,)),
            dma((2,)),
            dma((2,)),
            dma((2,)),
            dma((2,)),
            dma((2,)),
            dma((2,)),
            dma((4,)),
            dma((4,)),
            dma,
            dma,
            dma((3,)),
            dma((3,)),
            dma,
        ],
        compiler_params=pltpu.CompilerParams(
            collective_id=0, has_side_effects=True, vmem_limit_bytes=58 * 1024 * 1024
        ),
    )(
        responses[0], kl_terms[0], norm_gain.reshape(D // HD, HD), freq, w_qkv.reshape(D, 3 * HD),
        readout, slot_bin, entry_source, bin_segments,
    )
    return out.reshape(1, PIECES * BIN_DEV, HD), scores


def solution(mesh):
    placed = (
        P("dp", "tensor", None),
        P("dp", None, None),
        P(),
        P(None, "tensor", None),
        P("tensor", None),
        P("dp", None),
        P("dp", None),
        P("dp", None),
    )
    return jax.shard_map(
        body,
        mesh=mesh,
        in_specs=placed,
        out_specs=(P("dp", None, "tensor"), P("dp", None)),
        check_vma=False,
    )
```

```python
import jax
import jax.numpy as jnp
import numpy as np
from jax import lax
from jax.experimental import pallas as pl
from jax.experimental.pallas import tpu as pltpu
from jax.sharding import PartitionSpec as P

D = 4608
HD = 128
RESP = 8
CAP = 10
BIN_DEV = 64
LMAX = 160
PIECES = 16
NZ = 16
CHUNK = 16
ROWS = PIECES * CHUNK
LATE = 5
FOLD = D // 4
FOLD_LO = 640
MAIN = 256
EXTRA = 128

epsilon = 1e-06
beta_weight = 0.05
score_scale = 1.0 / 12.0
soft_cap = 50.0
rope_base = 10000.0

F32 = jnp.float32
BF16 = jnp.bfloat16
I32 = jnp.int32


def iota(shape, dim):
    return lax.broadcasted_iota(I32, shape, dim)


def slot_of(row):
    slot = jnp.zeros_like(row)
    for j in range(1, RESP):
        slot = slot + jnp.where(row >= CAP * j, 1, 0)
    return slot


def per_slot(slot, counts):
    out = jnp.zeros(slot.shape, I32)
    for j in range(RESP):
        out = jnp.where(slot == j, counts[j], out)
    return out


def kernel(
    resp, kl, gain, freq, w_hbm, readout, slot_bin, entry_source, bin_segments,
    out, scores,
    ge, gx, gl, nb, w, meta, cos_t, sin_t, low_t, high_t, code_t, qs, ks, vs,
    ib, ibx, io, iox, seli, os, zb, sel0, sel, ob0, ob, fo, rx, sc,
    w_sem, r1, r2, ag_send, meta_send, meta_recv, i_send, i_recv, ix_send, ix_recv,
    p1_send, p1_recv, sib_send, sib_recv, p2_send, p2_recv, rw_send, rw_recv, own_sem,
):
    d = lax.axis_index("dp")
    t = lax.axis_index("tensor")
    z, core = d // 2, d % 2
    y, x = t // 4, t % 4
    a = (1 - core) * x + core * y
    b = (1 - core) * y + core * x

    def piece(i, j):
        i, j = (a + i) % 4, (b + j) % 4
        return (1 - core) * (j * 4 + i) + core * (i * 4 + j)

    def in_z(target):
        return {"dp": target * 2 + core}

    sibling = {"dp": z * 2 + (1 - core)}

    def remote(src, dst, send, recv, device):
        return pltpu.make_async_remote_copy(
            src_ref=src, dst_ref=dst, send_sem=send, recv_sem=recv,
            device_id=device, device_id_type=pl.DeviceIdType.MESH,
        )

    def drain(ref, sem):
        pltpu.make_async_copy(ref, ref, sem).wait()

    def over_z(step):
        def body(i, carry):
            step((z + i) % NZ)
            return carry

        lax.fori_loop(1, NZ, body, 0)

    def over_plane(step):
        def body(i, carry):
            step((t + i) % PIECES)
            return carry

        lax.fori_loop(1, PIECES, body, 0)

    w_copy = pltpu.make_async_copy(w_hbm, w, w_sem)
    w_copy.start()
    barrier = pltpu.get_barrier_semaphore()

    def greet(device):
        pl.semaphore_signal(barrier, inc=1, device_id=device, device_id_type=pl.DeviceIdType.MESH)

    over_z(lambda target: greet(in_z(target)))
    over_plane(lambda target: greet({"tensor": target}))
    greet(sibling)

    lane = iota((1, HD), 1)
    meta[core, z] = jnp.full((8, HD), 99, I32)
    meta[core, z, 0:1, 0:BIN_DEV] = bin_segments[...]
    meta[core, z, 1:2, 0:RESP] = entry_source[...]

    gains = gain[...]
    gains = jnp.concatenate([gains[i:i + 1, :] for i in range(D // HD)], axis=1)
    for c in range(5):
        rows = resp[CHUNK * c:CHUNK * (c + 1), :].astype(F32)
        mean_square = jnp.sum(rows * rows, axis=-1, keepdims=True) * (1.0 / D)
        normed = (rows * lax.rsqrt(mean_square + epsilon) * gains).astype(BF16)
        if c < 3:
            ge[c, t] = normed
        else:
            nb[CHUNK * (c - 3):CHUNK * (c - 2), :] = normed
        if c == 3:
            wide = normed.astype(F32)
            block = iota((CHUNK, FOLD), 0) // 4
            folded = wide[:, 0:FOLD]
            for q in range(1, 4):
                part = pltpu.roll(wide[:, FOLD * q:FOLD * (q + 1)], 4 * q, 0)
                folded = jnp.where(block == q, part, folded)
            gx[t] = folded.astype(BF16)

    pl.semaphore_wait(barrier, PIECES - 1 + 1 + NZ - 1)

    up_a, down_a = {"tensor": piece(1, 0)}, {"tensor": piece(-1, 0)}
    up_b, down_b = {"tensor": piece(0, 1)}, {"tensor": piece(0, -1)}
    order = (0, -1, 1, 2)

    def view(c, p, part=None):
        if c == 3:
            cut = {None: pl.ds(0, FOLD), 0: pl.ds(0, FOLD_LO), 1: pl.ds(FOLD_LO, FOLD - FOLD_LO)}[part]
            return gx.at[p, :, cut]
        cut = {None: pl.ds(0, D), 0: pl.ds(0, D // 2), 1: pl.ds(D // 2, D // 2)}[part]
        if c < 3:
            return ge.at[c, p, :, cut]
        return gl.at[p, pl.ds(CHUNK * (c - 4), CHUNK), cut]

    def full(c, p, sem, device):
        return remote(view(c, p), view(c, p), ag_send.at[c], sem, device)

    def half(c, p, part, sem, device):
        return remote(view(c, p, part), view(c, p, part), ag_send.at[c], sem, device)

    def second_sends(c, i):
        p = piece(order[i], 0)
        full(c, p, r2.at[c, i, 0], up_b).start()
        full(c, p, r2.at[c, i, 1], down_b).start()

    def first_sends(c):
        full(c, t, r1.at[c, 0], up_a).start()
        full(c, t, r1.at[c, 1], down_a).start()

    def first_ring(c):
        full(c, piece(-1, 0), r1.at[c, 0], up_a).wait_recv()
        half(c, piece(-1, 0), 0, r1.at[c, 2], up_a).start()
        second_sends(c, 1)
        full(c, piece(1, 0), r1.at[c, 1], down_a).wait_recv()
        half(c, piece(1, 0), 1, r1.at[c, 3], down_a).start()
        second_sends(c, 2)
        half(c, piece(2, 0), 0, r1.at[c, 2], up_a).wait_recv()
        half(c, piece(2, 0), 1, r1.at[c, 3], down_a).wait_recv()
        second_sends(c, 3)

    def second_ring(c):
        for i in range(4):
            below, above = piece(order[i], -1), piece(order[i], 1)
            full(c, below, r2.at[c, i, 0], up_b).wait_recv()
            half(c, below, 0, r2.at[c, i, 2], up_b).start()
            full(c, above, r2.at[c, i, 1], down_b).wait_recv()
            half(c, above, 1, r2.at[c, i, 3], down_b).start()

    def second_end(c):
        for i in range(4):
            opposite = piece(order[i], 2)
            half(c, opposite, 0, r2.at[c, i, 2], up_b).wait_recv()
            half(c, opposite, 1, r2.at[c, i, 3], down_b).wait_recv()

    def half_cols(target, h):
        return pl.ds(pl.multiple_of(target * MAIN + h * EXTRA, EXTRA), EXTRA)

    def extra_cols(target):
        return pl.ds(pl.multiple_of(NZ * MAIN + (target // 4) * EXTRA, EXTRA), EXTRA)

    def spread(target, h):
        remote(nb.at[:, half_cols(target, h)], ib.at[h, core, z], i_send.at[h], i_recv.at[h], in_z(target)).start()

    def spread_extra(target):
        spread(target, 1)

        @pl.when(target % 4 == 0)
        def _():
            remote(nb.at[:, extra_cols(target)], ibx.at[core, z], ix_send.at[0], ix_recv.at[0], in_z(target)).start()

    def collect(target, h):
        remote(
            io.at[h, target], gl.at[t, :, half_cols(z, h)], i_send.at[2 + h], i_recv.at[2 + h], in_z(target)).start()

    def collect_extra(target):
        collect(target, 1)

        @pl.when(z % 4 == 0)
        def _():
            remote(iox.at[target], gl.at[t, :, extra_cols(z)], ix_send.at[1], ix_recv.at[1], in_z(target)).start()

    first_sends(3)
    second_sends(3, 0)
    first_sends(0)
    second_sends(0, 0)
    over_z(lambda target: spread(target, 0))
    first_sends(1)
    second_sends(1, 0)
    over_z(lambda target: remote(
        meta.at[core, z], meta.at[core, z], meta_send.at[0], meta_recv.at[0], in_z(target)).start())
    first_sends(2)
    over_z(spread_extra)
    for h in range(2):
        ib[h, core, z] = nb[:, half_cols(z, h)]

    @pl.when(z % 4 == 0)
    def _():
        ibx[core, z] = nb[:, extra_cols(z)]

    first_ring(3)
    first_ring(0)
    second_sends(2, 0)
    second_ring(3)

    drain(meta.at[core, pl.ds(0, NZ - 1)], meta_recv.at[0])
    meta_pass = remote(meta.at[core], meta.at[core], meta_send.at[1], meta_recv.at[1], sibling)
    meta_pass.start()

    def bin_rows(tile, start, size):
        seg_row = tile[0:1, :].astype(F32)
        src_row = tile[1:2, :].astype(F32)
        r_col = start + iota((size, HD), 0)
        l_row = iota((size, HD), 1)
        seg = jnp.sum(jnp.where(r_col == l_row, seg_row, 0.0), axis=1, keepdims=True)
        number = jnp.sum(jnp.where(seg_row == seg, 1.0, 0.0), axis=1, keepdims=True)
        offset = jnp.sum(jnp.where(seg_row < seg, 1.0, 0.0), axis=1, keepdims=True)
        source = jnp.sum(jnp.where(l_row.astype(F32) == seg, src_row, 0.0), axis=1, keepdims=True)
        source = source.astype(I32)
        within = r_col[:, 0:1].astype(F32) - offset
        return seg, number, within, (source & 1) * NZ + (source >> 1)

    def pick_late(i, carry):
        seg, _, within, place = bin_rows(meta[core, i], 32, 32)
        row = CAP * seg.astype(I32) + within.astype(I32) - 48
        column = jnp.where(seg >= LATE, place * 32 + row, -1)
        seli[i] = jnp.where(iota((32, 2 * NZ * 32), 1) == column, 1.0, 0.0).astype(BF16)
        return carry

    def late_tables():
        seg, number, within, _ = bin_rows(meta[core, z], 32, 32)
        for c in range(2):
            def spread_rows(col):
                col = col[CHUNK * c:CHUNK * (c + 1)].reshape(1, CHUNK, 1)
                return jnp.broadcast_to(col, (PIECES, CHUNK, HD)).reshape(ROWS, HD)

            slot = spread_rows(seg)
            position = (iota((ROWS, HD), 0) // CHUNK).astype(F32) * spread_rows(number) + spread_rows(within)
            angle = position * freq[...]
            cos_t[4 + c] = jnp.cos(angle)
            sine = jnp.sin(angle)
            sin_t[4 + c] = jnp.where(iota((ROWS, HD), 1) < HD // 2, -sine, sine)
            live = slot >= LATE
            low_t[c] = jnp.where(live, slot * LMAX, 4.0 * RESP * LMAX)
            high_t[c] = jnp.where(live, slot * LMAX + position, -1.0)
            code = jnp.where(live, slot * LMAX + position, 2.0 * RESP * LMAX)
            code_t[c] = jnp.transpose(code)[0:8, :]

    def pick_early(i, carry):
        seg, _, within, place = bin_rows(meta[core, i], 0, BIN_DEV)
        row = CAP * seg.astype(I32) + within.astype(I32)
        first = jnp.where((seg < LATE) & (row < 30), place * 32 + row, -1)
        second = jnp.where((seg < LATE) & (row >= 30), place * 32 + jnp.where(row < 32, row, row - 32), -1)
        spot = iota((BIN_DEV, 2 * NZ * 32), 1)
        sel0[i] = jnp.where(spot[0:32] == first[0:32], 1.0, 0.0).astype(BF16)
        sel[i] = jnp.where(spot == second, 1.0, 0.0).astype(BF16)
        return carry

    def pass_on(h):
        drain(ib.at[h, core, pl.ds(0, NZ - 1)], i_recv.at[h])
        remote(ib.at[h, core], ib.at[h, core], sib_send.at[2 + h], sib_recv.at[2 + h], sibling).start()

    def choose(h):
        remote(ib.at[h, 1 - core], ib.at[h, 1 - core], sib_send.at[2 + h], sib_recv.at[2 + h], sibling).wait_recv()
        picks = seli[...].reshape(NZ * 32, 2 * NZ * 32)
        rows = jnp.dot(picks, ib[h].reshape(2 * NZ * 32, EXTRA), preferred_element_type=F32)
        io[h] = rows.astype(BF16).reshape(NZ, 32, EXTRA)

    lax.fori_loop(0, NZ, pick_late, 0)
    pass_on(0)
    first_ring(1)
    choose(0)
    over_z(lambda target: collect(target, 0))
    pass_on(1)

    @pl.when(z % 4 == 0)
    def _():
        drain(ibx.at[core, pl.ds(0, NZ - 1)], ix_recv.at[0])
        remote(ibx.at[core], ibx.at[core], sib_send.at[4], sib_recv.at[4], sibling).start()

    second_ring(0)
    choose(1)

    @pl.when(z % 4 == 0)
    def _():
        remote(ibx.at[1 - core], ibx.at[1 - core], sib_send.at[4], sib_recv.at[4], sibling).wait_recv()
        picks = seli[...].reshape(NZ * 32, 2 * NZ * 32)
        rows = jnp.dot(picks, ibx[...].reshape(2 * NZ * 32, EXTRA), preferred_element_type=F32)
        iox[...] = rows.astype(BF16).reshape(NZ, 32, EXTRA)

    over_z(collect_extra)
    for h in range(2):
        gl[t, :, half_cols(z, h)] = io[h, z]

    @pl.when(z % 4 == 0)
    def _():
        gl[t, :, extra_cols(z)] = iox[z]

    second_end(3)
    first_ring(2)
    second_ring(1)

    def rotated(raw, c):
        def rotate(part):
            part = part.astype(F32)
            turned = part * cos_t[c] + pltpu.roll(part, HD // 2, 1) * sin_t[c]
            return turned.astype(BF16)

        qs[c] = rotate(raw[:, 0:HD])
        ks[c] = rotate(raw[:, HD:2 * HD])
        vs[c] = raw[:, 2 * HD:3 * HD]

    def project(c):
        rows = ge[c] if c < 3 else gl[:, CHUNK * (c - 4):CHUNK * (c - 3), :]
        raw = jnp.dot(rows.reshape(ROWS, D), w[...], preferred_element_type=F32)
        rotated(raw.astype(BF16), c)

    def project_folded():
        rows = gx[...].reshape(ROWS, FOLD)
        raw = jnp.dot(rows, w[0:FOLD, :], preferred_element_type=F32)
        for q in range(1, 4):
            part = jnp.dot(rows, w[FOLD * q:FOLD * (q + 1), :], preferred_element_type=F32)
            raw = raw + pltpu.roll(part, ROWS - 4 * q, 0)
        rotated(raw.astype(BF16), 3)

    def softmax_values(q, low, high, keys):
        es = []
        for ck, code in keys:
            s = lax.dot_general(q, ks[ck], (((1,), (1,)), ((), ())), preferred_element_type=F32)
            capped = soft_cap * jnp.tanh(s * (score_scale / soft_cap))
            allowed = (code >= low) & (code <= high)
            es.append(jnp.where(allowed, jnp.exp(capped), 0.0))
        total = sum(jnp.sum(e, axis=-1, keepdims=True) for e in es)
        inverse = 1.0 / jnp.maximum(total, 1e-30)
        result = jnp.zeros((q.shape[0], HD), F32)
        for (ck, _), e in zip(keys, es):
            result = result + jnp.dot((e * inverse).astype(BF16), vs[ck], preferred_element_type=F32)
        return result.astype(BF16)

    in_chunk = iota((ROWS, 1), 0) % CHUNK

    def attend(q, row, first, count):
        index = iota((ROWS, 1), 0)
        slot = slot_of(row)
        low = slot * LMAX
        high = low + (index // CHUNK) * CAP + row - CAP * slot
        keys = []
        for ck in range(first, first + count):
            kidx = iota((1, ROWS), 1)
            krow = CHUNK * ck + kidx % CHUNK
            kslot = slot_of(krow)
            within = krow - CAP * kslot
            code = kslot * LMAX + (kidx // CHUNK) * CAP + within
            live = (within < per_slot(kslot, counts)) & (kslot < LATE)
            keys.append((ck, jnp.where(live, code, 2 * RESP * LMAX)))
        return softmax_values(q, low, high, keys).reshape(PIECES, CHUNK, HD)

    def to_pieces(k):
        over_z(lambda target: remote(
            os.at[k, target], zb.at[k, core, z], p1_send.at[k], p1_recv.at[k], in_z(target)).start())
        zb[k, core, z] = os[k, z]

    def share(k):
        drain(zb.at[k, core, pl.ds(0, NZ - 1)], p1_recv.at[k])
        remote(zb.at[k, core], zb.at[k, core], sib_send.at[k], sib_recv.at[k], sibling).start()

    def shared(k):
        remote(zb.at[k, 1 - core], zb.at[k, 1 - core], sib_send.at[k], sib_recv.at[k], sibling).wait_recv()

    def late_keys():
        return [(4, code_t[0, 0:1, :]), (5, code_t[1, 0:1, :])]

    remote(meta.at[1 - core], meta.at[1 - core], meta_send.at[1], meta_recv.at[1], sibling).wait_recv()

    every = meta[...].reshape(2 * NZ, 8, HD)
    tile_row = iota((2 * NZ, 8, HD), 1)
    tile_id = iota((2 * NZ, 8, HD), 0)
    tile_bin = (tile_id % NZ) * 2 + tile_id // NZ
    is_segment = tile_row == 0
    counts = []
    for j in range(RESP):
        hit = is_segment & (every == j) & (tile_bin == slot_bin[0:1, j:j + 1].reshape(1, 1, 1))
        counts.append(jnp.sum(jnp.where(hit, 1.0, 0.0)).astype(I32))

    def rope_tables(c, carry):
        index = iota((ROWS, HD), 0)
        row = CHUNK * c + index % CHUNK
        slot = slot_of(row)
        position = (index // CHUNK) * per_slot(slot, counts) + row - CAP * slot
        angle = position.astype(F32) * freq[...]
        cos_t[c] = jnp.cos(angle)
        sine = jnp.sin(angle)
        sin_t[c] = jnp.where(iota((ROWS, HD), 1) < HD // 2, -sine, sine)
        return carry

    lax.fori_loop(0, 4, rope_tables, 0)
    w_copy.wait()
    late_tables()
    project_folded()
    second_end(0)
    project(0)
    second_ring(2)

    lax.fori_loop(0, NZ, pick_early, 0)
    for h in range(2):
        drain(io.at[h, pl.ds(0, NZ - 1)], i_recv.at[2 + h])

    @pl.when(z % 4 == 0)
    def _():
        drain(iox.at[pl.ds(0, 3)], ix_recv.at[1])

    @pl.when(z % 4 != 0)
    def _():
        drain(iox.at[pl.ds(0, 4)], ix_recv.at[1])

    first_sends(4)
    second_sends(4, 0)
    first_sends(5)
    second_sends(5, 0)
    second_end(1)
    project(1)
    os[0, :, 0:CHUNK, :] = attend(qs[0], in_chunk, 0, 2)
    os[0, :, CHUNK:32, :] = attend(qs[1], CHUNK + in_chunk, 0, 2)
    to_pieces(0)
    second_end(2)
    project(2)
    os[1, :, 0:CHUNK, :] = attend(qs[2], 2 * CHUNK + in_chunk, 1, 3)
    behind = in_chunk >= CHUNK - 2
    mixed = jnp.where(behind, qs[1].astype(F32), qs[3].astype(F32)).astype(BF16)
    row = in_chunk + jnp.where(behind, CHUNK, 3 * CHUNK)
    os[1, :, CHUNK:32, :] = attend(mixed, row, 1, 3)
    to_pieces(1)
    first_ring(4)
    first_ring(5)
    share(0)
    second_ring(4)

    weights = readout[...].astype(F32)
    last_row = jnp.full((1, HD), -1, I32)
    penalty = jnp.zeros((1, HD), F32)
    token = iota((1, LMAX), 1)
    for j in range(RESP):
        if j < LATE:
            last_row = jnp.where(lane == j, CAP * j + counts[j] - 1, last_row)
        live = jnp.where(token < counts[j] * PIECES, kl[j:j + 1, :].astype(F32), 0.0)
        penalty = jnp.where(lane == j, jnp.sum(live, axis=1, keepdims=True), penalty)

    def reward_of(rows, row, wanted):
        value = jnp.sum(rows.astype(F32) * weights, axis=1, keepdims=True)
        return jnp.sum(jnp.where(row == wanted, value, 0.0), axis=0, keepdims=True)

    place = iota((32, 1), 0)
    reward = reward_of(os[0, PIECES - 1], jnp.where(place < 30, place, -5), last_row)
    reward = reward + reward_of(os[1, PIECES - 1], jnp.where(place < 30, 32 + place, place), last_row)

    reward = reward - jnp.where(t == 0, beta_weight, 0.0) * penalty
    sc[core, z] = jnp.broadcast_to(reward, (8, HD))
    over_z(lambda target: remote(
        sc.at[core, z], sc.at[core, z], rw_send.at[1], rw_recv.at[1], in_z(target)).start())
    shared(0)
    src = zb[0].reshape(2 * NZ * 32, HD)
    rows = jnp.dot(sel0[...].reshape(NZ * 32, 2 * NZ * 32), src, preferred_element_type=F32)
    ob0[...] = rows.reshape(NZ, 32, HD)
    share(1)
    shared(1)
    src = zb[1].reshape(2 * NZ * 32, HD)
    rows = jnp.dot(sel[...].reshape(NZ * BIN_DEV, 2 * NZ * 32), src, preferred_element_type=F32)
    rows = rows.reshape(NZ, BIN_DEV, HD)
    ob[:, 0:32, :] = (rows[:, 0:32] + ob0[...]).astype(BF16)
    ob[:, 32:64, :] = rows[:, 32:64].astype(BF16)
    over_z(lambda target: remote(
        ob.at[target], fo.at[z], p2_send, p2_recv, in_z(target)).start())
    fo[z] = ob[z]

    second_ring(5)
    drain(sc.at[core, pl.ds(0, NZ - 1)], rw_recv.at[1])
    sc_pass = remote(sc.at[core], sc.at[core], rw_send.at[2], rw_recv.at[2], sibling)
    sc_pass.start()

    seg_row = meta[core, z, 0:1, :]
    late_last = jnp.full((1, HD), -1, I32)
    for j in range(LATE, RESP):
        upto = jnp.sum(jnp.where(seg_row <= j, 1.0, 0.0), axis=1, keepdims=True).astype(I32)
        late_last = jnp.where(lane == j, upto - 33, late_last)

    second_end(4)
    project(4)
    remote(sc.at[1 - core], sc.at[1 - core], rw_send.at[2], rw_recv.at[2], sibling).wait_recv()
    all_scores = sc[...].reshape(2 * NZ, 8, HD)
    sources = jnp.full((1, HD), -1, I32)
    for j in range(RESP):
        sources = jnp.where(lane == j, entry_source[0:1, j:j + 1], sources)
    mine = (tile_bin == sources.reshape(1, 1, HD)) & is_segment
    picked = jnp.sum(jnp.where(mine, all_scores, 0.0), axis=0)
    picked = jnp.sum(picked, axis=0, keepdims=True)

    second_end(5)
    project(5)
    tail = pl.ds(ROWS - CHUNK, CHUNK)
    q_last = jnp.concatenate([qs[4, tail, :], qs[5, tail, :]], axis=0)
    low = jnp.concatenate([low_t[0, tail, 0:1], low_t[1, tail, 0:1]], axis=0)
    high = jnp.concatenate([high_t[0, tail, 0:1], high_t[1, tail, 0:1]], axis=0)
    last_rows = softmax_values(q_last, low, high, late_keys())
    rx[t] = jnp.broadcast_to(picked + reward_of(last_rows, place, late_last), (8, HD))
    over_plane(lambda target: remote(
        rx.at[t], rx.at[t], rw_send.at[0], rw_recv.at[0], {"tensor": target}).start())
    late = []
    late.append(softmax_values(qs[4], low_t[0, :, 0:1], high_t[0, :, 0:1], late_keys()))
    late.append(softmax_values(qs[5], low_t[1, :, 0:1], high_t[1, :, 0:1], late_keys()))

    drain(ob.at[pl.ds(0, NZ - 1)], p2_recv)
    for c in range(2):
        rows = pl.ds(32 + CHUNK * c, CHUNK)
        mine = late[c].reshape(PIECES, CHUNK, HD).astype(F32)
        fo[:, rows, :] = (fo[:, rows, :].astype(F32) + mine).astype(BF16)
    out_copy = pltpu.make_async_copy(fo, out, own_sem)
    out_copy.start()

    for c in range(6):
        if c < 3:
            sent = ge.at[c, pl.ds(0, 15)]
        elif c == 3:
            sent = gx.at[pl.ds(0, 15)]
        else:
            sent = gl.at[pl.ds(0, 15), pl.ds(CHUNK * (c - 4), CHUNK)]
        drain(sent, ag_send.at[c])
    for h in range(4):
        drain(io.at[0, pl.ds(0, NZ - 1)], i_send.at[h])

    @pl.when(z % 4 == 0)
    def _():
        drain(iox.at[pl.ds(0, 3)], ix_send.at[0])
        drain(iox.at[pl.ds(0, NZ - 1)], ix_send.at[1])
        drain(ibx.at[core], sib_send.at[4])

    @pl.when(z % 4 != 0)
    def _():
        drain(iox.at[pl.ds(0, 4)], ix_send.at[0])

    for k in range(2):
        drain(os.at[k, pl.ds(0, NZ - 1)], p1_send.at[k])
        drain(zb.at[k, core], sib_send.at[k])
    for h in range(2):
        drain(ib.at[h, core], sib_send.at[2 + h])
    drain(ob.at[pl.ds(0, NZ - 1)], p2_send)
    drain(meta.at[core, pl.ds(0, NZ - 1)], meta_send.at[0])
    drain(meta.at[core], meta_send.at[1])
    drain(sc.at[core, pl.ds(0, NZ - 1)], rw_send.at[1])
    drain(sc.at[core], rw_send.at[2])
    drain(rx.at[pl.ds(0, PIECES - 1)], rw_recv.at[0])
    scores[...] = jnp.sum(rx[...], axis=0)[0:1, 0:RESP]
    drain(rx.at[pl.ds(0, PIECES - 1)], rw_send.at[0])
    out_copy.wait()


def body(responses, kl_terms, norm_gain, w_qkv, readout, slot_bin, entry_source, bin_segments):
    steps = np.arange(HD // 2, dtype=np.float32)
    frequency = (np.float32(rope_base) ** (-2.0 * steps / HD)).astype(np.float32)
    freq = jnp.asarray(np.concatenate([frequency, frequency])[None, :])
    vmem = pl.BlockSpec(memory_space=pltpu.VMEM)
    hbm = pl.BlockSpec(memory_space=pl.ANY)
    dma = pltpu.SemaphoreType.DMA
    out, scores = pl.pallas_call(
        kernel,
        out_shape=(
            jax.ShapeDtypeStruct((PIECES, BIN_DEV, HD), BF16),
            jax.ShapeDtypeStruct((1, RESP), F32),
        ),
        in_specs=[vmem, vmem, vmem, vmem, hbm, vmem, vmem, vmem, vmem],
        out_specs=(hbm, vmem),
        scratch_shapes=[
            pltpu.VMEM((3, PIECES, CHUNK, D), BF16),
            pltpu.VMEM((PIECES, CHUNK, FOLD), BF16),
            pltpu.VMEM((PIECES, 2 * CHUNK, D), BF16),
            pltpu.VMEM((2 * CHUNK, D), BF16),
            pltpu.VMEM((D, 3 * HD), BF16),
            pltpu.VMEM((2, NZ, 8, HD), I32),
            pltpu.VMEM((6, ROWS, HD), F32),
            pltpu.VMEM((6, ROWS, HD), F32),
            pltpu.VMEM((2, ROWS, HD), F32),
            pltpu.VMEM((2, ROWS, HD), F32),
            pltpu.VMEM((2, 8, ROWS), F32),
            pltpu.VMEM((6, ROWS, HD), BF16),
            pltpu.VMEM((6, ROWS, HD), BF16),
            pltpu.VMEM((6, ROWS, HD), BF16),
            pltpu.VMEM((2, 2, NZ, 32, EXTRA), BF16),
            pltpu.VMEM((2, NZ, 32, EXTRA), BF16),
            pltpu.VMEM((2, NZ, 32, EXTRA), BF16),
            pltpu.VMEM((NZ, 32, EXTRA), BF16),
            pltpu.VMEM((NZ, 32, 2 * NZ * 32), BF16),
            pltpu.VMEM((2, PIECES, 32, HD), BF16),
            pltpu.VMEM((2, 2, NZ, 32, HD), BF16),
            pltpu.VMEM((NZ, 32, 2 * NZ * 32), BF16),
            pltpu.VMEM((NZ, BIN_DEV, 2 * NZ * 32), BF16),
            pltpu.VMEM((NZ, 32, HD), F32),
            pltpu.VMEM((NZ, BIN_DEV, HD), BF16),
            pltpu.VMEM((PIECES, BIN_DEV, HD), BF16),
            pltpu.VMEM((PIECES, 8, HD), F32),
            pltpu.VMEM((2, NZ, 8, HD), F32),
            dma,
            dma((6, 4)),
            dma((6, 4, 4)),
            dma((6,)),
            dma((2,)),
            dma((2,)),
            dma((4,)),
            dma((4,)),
            dma((2,)),
            dma((2,)),
            dma((2,)),
            dma((2,)),
            dma((5,)),
            dma((5,)),
            dma,
            dma,
            dma((3,)),
            dma((3,)),
            dma,
        ],
        compiler_params=pltpu.CompilerParams(
            collective_id=0, has_side_effects=True, vmem_limit_bytes=58 * 1024 * 1024
        ),
    )(
        responses[0], kl_terms[0], norm_gain.reshape(D // HD, HD), freq, w_qkv.reshape(D, 3 * HD),
        readout, slot_bin, entry_source, bin_segments,
    )
    return out.reshape(1, PIECES * BIN_DEV, HD), scores


def solution(mesh):
    placed = (
        P("dp", "tensor", None),
        P("dp", None, None),
        P(),
        P(None, "tensor", None),
        P("tensor", None),
        P("dp", None),
        P("dp", None),
        P("dp", None),
    )
    return jax.shard_map(
        body,
        mesh=mesh,
        in_specs=placed,
        out_specs=(P("dp", None, "tensor"), P("dp", None)),
        check_vma=False,
    )
```
